32 devices in a mesh: dp: 8 (over z, y), chan: 4 (over x, core).
Axes of the slice: x: 2, y: 2, z: 4, core: 2. Of those that a mesh axis runs over, the one named last changes fastest.
Arguments:
- big_input: float32 [8, 48, 4, 9216], P('dp', 'chan'), may hold values from -6 to 6
- small_input: float32 [8, 48, 4, 4096], P('dp', 'chan'), may hold values from -6 to 6
- spectral_weight: float32 [2, 48, 48, 4, 512], P(None, 'chan'), may hold values from -0.3125 to 0.3125
- point_weight: float32 [48, 48, 4], P('chan'), may hold values from -0.4375 to 0.4375
- point_bias: float32 [48, 4], P('chan'), may hold values from -3 to 3
- big_cotangent: float32 [8, 48, 4, 9216], P('dp', 'chan'), may hold values from -6 to 6
- small_cotangent: float32 [8, 48, 4, 4096], P('dp', 'chan'), may hold values from -6 to 6
- big_live: int32 [8], P('dp'), may hold values from 0 to 1, as said below
- small_live: int32 [8], P('dp'), may hold values from 0 to 1, as said below
Outputs:
- big_out: float32 [8, 48, 4, 9216], P('dp', 'chan')
- small_out: float32 [8, 48, 4, 4096], P('dp', 'chan')
- big_grad: float32 [8, 48, 4, 9216], P('dp', 'chan')
- small_grad: float32 [8, 48, 4, 4096], P('dp', 'chan')
- spectral_grad: float32 [2, 48, 48, 4, 512], P(None, 'chan')
- point_grad: float32 [48, 48, 4], P('chan')
- bias_grad: float32 [48, 4], P('chan')
The draws below stay inside these ranges and needn't reach their ends.
Inputs may be any that keep to these rules, and one draw needn't show every extreme that they name: `big_live`: each index of dp holds 1 consecutive entries; in every draw one index of dp has all its entries equal to 1. `small_live`: each index of dp holds 1 consecutive entries; in every draw one index of dp has all its entries equal to 1.
All inputs are finite; a program needn't handle non-finite values.
Results may differ from the reference program's by a relative error of at most 0.0003.
Values sent between devices are 32-bit elements; how exact they have to be, the bound alone decides.
A program may use at most 384 MiB of HBM per device.

```python
import math
import jax
import jax.numpy as jnp
from jax import lax

CH = 48
M = 16
HB = 96
HS = 64
BIG_DEV = 1
SMALL_DEV = 1
MODES = 512
NB = 8
NS = 8
SAMPLES = 16
PIXELS = 106496


def slot_flags(key, slot_count, per_device):
    random_flags = (jax.random.randint(key, (slot_count,), 0, 4) > 0).astype(jnp.int32)
    chosen = jax.random.randint(jax.random.fold_in(key, 11), (), 0, slot_count // per_device)
    owner_device = jnp.arange(slot_count) // per_device
    return jnp.where(owner_device == chosen, 1, random_flags).astype(jnp.int32)


def draw_big_live(key, part):
    key = jax.random.fold_in(key, 3)
    return slot_flags(key, NB, BIG_DEV)


def draw_small_live(key, part):
    key = jax.random.fold_in(key, 5)
    return slot_flags(key, NS, SMALL_DEV)


def levels(own_key, dims, shards, least, high):
    level, own = 1.0, jax.random.fold_in(own_key, 6)
    for dim, blocks in shards:
        draws = jnp.exp(jax.random.uniform(jax.random.fold_in(own, dim), (blocks,), jnp.float32, least / len(shards), high / len(shards)))
        level = level * jnp.repeat(draws, dims[dim] // blocks).reshape([-1 if axis == dim else 1 for axis in range(len(dims))])
    return level


def scatter_about(rng, dims, deviation, limit, split=(), held_as=jnp.bfloat16):
    level = levels(rng, dims, split, -0.22, 0.18) if split else 1.0
    drawn = jax.random.normal(rng, dims, jnp.float32) * deviation * level
    return jnp.minimum(jnp.maximum(drawn, -limit), limit).astype(held_as)


def setup_inputs(seed: int = 0) -> dict:
    streams_of = jax.random.split(jax.random.key(seed), 10)
    big_input = scatter_about(streams_of[0], (NB, CH, 4, HB * HB), 1.0, 6.0, ((0, 8), (1, 4)), jnp.float32)
    small_input = scatter_about(streams_of[1], (NS, CH, 4, HS * HS), 1.0, 6.0, ((0, 8), (1, 4)), jnp.float32)
    spectral_weight = scatter_about(streams_of[2], (2, CH, CH, 4, MODES), (8 * CH) ** -0.5, 0.3125, ((1, 4),), jnp.float32)
    point_weight = scatter_about(streams_of[3], (CH, CH, 4), (4 * CH) ** -0.5, 0.4375, ((0, 4),), jnp.float32)
    point_bias = scatter_about(streams_of[4], (CH, 4), 0.5, 3.0, ((0, 4),), jnp.float32)
    big_cotangent = scatter_about(streams_of[5], (NB, CH, 4, HB * HB), 1.0, 6.0, ((0, 8), (1, 4)), jnp.float32)
    small_cotangent = scatter_about(streams_of[6], (NS, CH, 4, HS * HS), 1.0, 6.0, ((0, 8), (1, 4)), jnp.float32)
    big_live = draw_big_live(jax.random.fold_in(streams_of[9], 71), 0)
    small_live = draw_small_live(jax.random.fold_in(streams_of[9], 71), 0)
    return {"big_input": big_input, "small_input": small_input, "spectral_weight": spectral_weight, "point_weight": point_weight, "point_bias": point_bias, "big_cotangent": big_cotangent, "small_cotangent": small_cotangent, "big_live": big_live, "small_live": small_live}


@jax.custom_vjp
def low(v):
    return lax.optimization_barrier(v.astype(jnp.bfloat16)).astype(jnp.float32)

@jax.custom_vjp
def low_back(v):
    return v

def low_keep(v):
    return (low(v), None)

def low_pass(kept, grad):
    return (grad,)

def back_keep(v):
    return (v, None)

def back_low(kept, grad):
    return (low(grad),)
low.defvjp(low_keep, low_pass)
low_back.defvjp(back_keep, back_low)
highest = lax.Precision.HIGHEST
blade_index = ((0, 1, 2, 3), (1, 0, 3, 2), (2, 3, 0, 1), (3, 2, 1, 0))
blade_sign = ((1.0, 1.0, 1.0, -1.0), (1.0, 1.0, 1.0, -1.0), (1.0, -1.0, 1.0, 1.0), (1.0, -1.0, 1.0, 1.0))

def clifford_dense(kernel):
    outer_list = []
    for out_blade in range(4):
        inner_list = [blade_sign[out_blade][in_blade] * kernel[:, :, blade_index[out_blade][in_blade]] for in_blade in range(4)]
        outer_list.append(jnp.stack(inner_list, axis=2))
    dense_stack = jnp.stack(outer_list, axis=1)
    dense_shape = dense_stack.shape
    return dense_stack.reshape((dense_shape[0] * 4, dense_shape[2] * 4) + dense_shape[4:])

def spectral_branch(field, spectral_weight, grid_side):
    batch_size = field.shape[0]
    planes = field.reshape(batch_size, CH * 4, grid_side, grid_side)
    spectrum = jnp.fft.rfft2(planes) / math.sqrt(grid_side * grid_side)
    kept_modes = jnp.concatenate([spectrum[:, :, :M, :M], spectrum[:, :, grid_side - M:, :M]], axis=2).reshape(batch_size, CH * 4, MODES)
    kept_real = jnp.real(kept_modes)
    kept_imaginary = jnp.imag(kept_modes)
    dense_real = clifford_dense(spectral_weight[0])
    dense_imaginary = clifford_dense(spectral_weight[1])
    mixed_real = jnp.einsum('ojk,bjk->bok', dense_real, kept_real, precision=highest) - jnp.einsum('ojk,bjk->bok', dense_imaginary, kept_imaginary, precision=highest)
    mixed_imaginary = jnp.einsum('ojk,bjk->bok', dense_real, kept_imaginary, precision=highest) + jnp.einsum('ojk,bjk->bok', dense_imaginary, kept_real, precision=highest)
    mixed_modes = lax.complex(mixed_real, mixed_imaginary).reshape(batch_size, CH * 4, 2 * M, M)
    zero_rows = jnp.zeros((batch_size, CH * 4, grid_side - 2 * M, M), mixed_modes.dtype)
    rows_full = jnp.concatenate([mixed_modes[:, :, :M], zero_rows, mixed_modes[:, :, M:]], axis=2)
    padded = jnp.pad(rows_full, ((0, 0), (0, 0), (0, 0), (0, grid_side // 2 + 1 - M)))
    field_out = jnp.fft.irfft2(padded, s=(grid_side, grid_side)) * (grid_side * grid_side / (2.0 * M))
    return field_out.reshape(batch_size, CH * 4, grid_side * grid_side)

def point_branch(flat_field, point_weight, point_bias):
    dense_point = clifford_dense(point_weight)
    mixed_sum = jnp.einsum('oj,bjp->bop', dense_point, flat_field, precision=highest)
    return mixed_sum + point_bias.reshape(CH * 4)[None, :, None]

def clifford_layer(field, spectral_weight, point_weight, point_bias, grid_side):
    batch_size = field.shape[0]
    flat_field = field.reshape(batch_size, CH * 4, grid_side * grid_side)
    spectral_part = spectral_branch(field, spectral_weight, grid_side)
    point_part = point_branch(flat_field, point_weight, point_bias)
    return (flat_field + jax.nn.gelu(spectral_part + point_part, approximate=False)).reshape(field.shape)

def reference(big_input, small_input, spectral_weight, point_weight, point_bias, big_cotangent, small_cotangent, big_live, small_live):
    hidden_big = clifford_layer(big_input, spectral_weight, point_weight, point_bias, HB)
    hidden_small = clifford_layer(small_input, spectral_weight, point_weight, point_bias, HS)

    def trained(field_big, field_small, spec_kernel, point_kernel, bias_vector):
        return (clifford_layer(field_big, spec_kernel, point_kernel, bias_vector, HB), clifford_layer(field_small, spec_kernel, point_kernel, bias_vector, HS))
    outputs, pullback = jax.vjp(trained, hidden_big, hidden_small, spectral_weight, point_weight, point_bias)
    mask_big = big_live.astype(jnp.float32)[:, None, None, None]
    mask_small = small_live.astype(jnp.float32)[:, None, None, None]
    gradients = pullback((big_cotangent * mask_big, small_cotangent * mask_small))
    spectral_scale = 1.0 / math.sqrt(SAMPLES)
    pixel_scale = 1.0 / math.sqrt(PIXELS)
    return (outputs[0], outputs[1], gradients[0], gradients[1], gradients[2] * spectral_scale, gradients[3] * pixel_scale, gradients[4] * pixel_scale)
```

```python
import functools
import math

import jax
import jax.numpy as jnp
import ml_dtypes
import numpy as np
from jax import lax
from jax.experimental import pallas as pl
from jax.experimental.pallas import tpu as pltpu
from jax.sharding import PartitionSpec as P

M = 16
MODES = 2 * M * M
HB = 96
HS = 64
CB = HB // 8
CS = HS // 8
LB = 8 * HB
LS = 8 * HS
NB = HB * HB // 4
NS = HS * HS // 4
NQ = NB + NS
TILES = 4
NEAR = 5
PG = 384
VMEM_LIMIT = 62 * 1024 * 1024

def mode_numbers():
    mode = np.arange(MODES)
    row = mode // M
    return np.where(row < M, row, row - 2 * M), mode % M


def pair_of(table):
    high = table.astype(ml_dtypes.bfloat16)
    return high, (table - high.astype(np.float64)).astype(ml_dtypes.bfloat16)


def column_table(side):
    cell, out = np.arange(8 * side), np.arange(8 * M)
    angle = np.outer(cell % side, out % M) % side * (2.0 * np.pi / side)
    same = np.equal.outer(cell // side, out // M)
    return np.concatenate([np.cos(angle) * same, -np.sin(angle) * same], axis=1)


def row_table(side):
    k, l = mode_numbers()
    row = np.arange(8 * M)
    angle = np.outer(row // M, k) % side * (2.0 * np.pi / side)
    same = np.equal.outer(row % M, l)
    cos, sin = np.cos(angle) * same, np.sin(angle) * same
    real = np.concatenate([cos, sin], axis=0).reshape(2 * 8 * M, TILES, 128)
    imag = np.concatenate([-sin, cos], axis=0).reshape(2 * 8 * M, TILES, 128)
    return np.stack([real, imag], axis=2).reshape(2 * 8 * M, 2 * MODES)


def chunk_phase(side, kind):
    k, l = mode_numbers()
    chunk = np.arange(side // 8)
    angle = (np.outer(8 * chunk, k) % side) * (2.0 * np.pi / side)
    scale = 1.0 / side if kind == "in" else np.where(l == 0, 1.0, 2.0) / (2.0 * M)
    return np.stack([np.cos(angle) * scale, np.sin(angle) * scale], axis=1).astype(np.float32)


def interleave(channels):
    table = np.zeros((4, 128, 256), ml_dtypes.bfloat16)
    for blade in range(4):
        for channel in range(channels):
            table[blade, channel, 4 * channel + blade] = 1
    return table


def split(value):
    high = value.astype(jnp.bfloat16)
    return high, (value - high.astype(jnp.float32)).astype(jnp.bfloat16)


def dot3(ah, al, bh, bl, dims=(((1,), (0,)), ((), ()))):
    dot = functools.partial(lax.dot_general, dimension_numbers=dims, preferred_element_type=jnp.float32)
    return dot(ah, bh) + (dot(ah, bl) + dot(al, bh))


NT = (((1,), (1,)), ((), ()))


def first_stage(h, l, th, tl, yh, yl, used):
    yh[used, :], yl[used, :] = split(dot3(h, l, th[...], tl[...]))


def forward_tile(yh, yl, vh, vl, phase, chunk0, count, rows, t):
    cols = pl.ds(pl.multiple_of(256 * t, 256), 256)
    used = slice(0, count * rows)
    local = dot3(yh[used, :], yl[used, :], vh[:, cols], vl[:, cols])
    lanes = pl.ds(pl.multiple_of(128 * t, 128), 128)
    re = im = None
    for j in range(count):
        lr = local[rows * j : rows * (j + 1), :128]
        li = local[rows * j : rows * (j + 1), 128:]
        cos = phase[chunk0 + j, 0:1, lanes]
        sin = phase[chunk0 + j, 1:2, lanes]
        pr = lr * cos + li * sin
        pi = li * cos - lr * sin
        re, im = (pr, pi) if re is None else (re + pr, im + pi)
    return re, im


def turn_modes(z_ref, zh, zl, phase, chunk, s, rows, row0):
    def tile(t, _):
        lanes = pl.ds(pl.multiple_of(128 * t, 128), 128)
        zr = z_ref[t, :, 256 * s : 256 * s + 128]
        zi = z_ref[t, :, 256 * s + 128 : 256 * s + 256]
        cos = phase[chunk, 0:1, lanes]
        sin = phase[chunk, 1:2, lanes]
        for part, value in enumerate((zr * cos - zi * sin, zr * sin + zi * cos)):
            high, low = split(value)
            where = pl.ds(pl.multiple_of(256 * t + 128 * part, 128), 128)
            zh[row0 : row0 + rows, where] = high
            zl[row0 : row0 + rows, where] = low
        return 0

    lax.fori_loop(0, TILES, tile, 0)


class Lanes:
    def __init__(self):
        sub = lax.broadcasted_iota(jnp.int32, (8, 128), 0)
        self.sub, self.s4 = sub, sub % 4
        self.even = sub % 2 == 0
        self.low = sub % 4 < 2
        self.half = sub < 4
        self.sign = jnp.where(self.even, 1.0, -1.0).astype(jnp.float32)
        self.sign_own = jnp.where(self.s4 == 1, -1.0, 1.0).astype(jnp.float32)
        self.sign_other = jnp.where(self.s4 == 2, -1.0, 1.0).astype(jnp.float32)
        self.by = {k: jnp.bitwise_xor(sub, k) for k in (1, 2, 3, 4)}

    def swap(self, x, k):
        return jnp.take_along_axis(x, self.by[k], axis=0)

    def to_matrix(self, x):
        return x * self.sign + self.swap(x, 1)

    def to_entries(self, x):
        return x * self.sign_own + self.swap(x, 1) * self.sign_other

    def columns(self, m):
        m3 = self.swap(m, 3)
        return jnp.where(self.even, m, m3), jnp.where(self.even, m3, m)


def mix_tile(wm, t, load, z_ref, me, xe, ln):
    groups = xe.shape[3] // 8
    outs = wm.shape[2]

    def expand(g, _):
        rows = pl.ds(pl.multiple_of(8 * g, 8), 8)
        for s in range(2):
            parts = []
            for ri in range(2):
                lanes = slice(256 * s + 128 * ri, 256 * s + 128 * ri + 128)
                parts.append(ln.columns(load(rows, lanes)))
            for c in range(2):
                xe[s, c, 0, rows, :] = parts[0][c]
                xe[s, c, 1, rows, :] = parts[1][c]
                xe[s, c, 2, rows, :] = parts[0][c] + parts[1][c]
        return 0

    lax.fori_loop(0, groups, expand, 0)

    def pair(p, _):
        acc = {}
        for g in range(groups):
            rows = slice(8 * g, 8 * g + 8)
            w = []
            for a in range(2):
                wr, wi = wm[t, 0, 2 * p + a, rows, :], wm[t, 1, 2 * p + a, rows, :]
                w.append((wr, wi, wr + wi))
            for s in range(2):
                for c in range(2):
                    for q in range(3):
                        x = xe[s, c, q, rows, :]
                        for a in range(2):
                            key = (a, s, c, q)
                            acc[key] = w[a][q] * x + acc[key] if key in acc else w[a][q] * x
        rows = pl.ds(pl.multiple_of(4 * outs * me + 8 * p, 8), 8)
        for s in range(2):
            for ri in range(2):
                out = []
                for a in range(2):
                    red = []
                    for c in range(2):
                        t1, t2, t3 = (acc[a, s, c, q] for q in range(3))
                        value = t1 - t2 if ri == 0 else t3 - t1 - t2
                        value = value + ln.swap(value, 4)
                        red.append(value + ln.swap(value, 2))
                    first = jnp.where(ln.low, red[0], red[1])
                    first = jnp.where(ln.even, first, ln.swap(first, 1))
                    second = jnp.where(ln.low, red[1], red[0])
                    second = jnp.where(ln.even, ln.swap(second, 1), second)
                    out.append(0.5 * (first + ln.sign * second))
                z_ref[t, rows, 256 * s + 128 * ri : 256 * s + 128 * ri + 128] = jnp.where(ln.half, out[0], out[1])
        return 0

    lax.fori_loop(0, outs // 2, pair, 0)


def both_outputs(d, ln):
    turned = ln.swap(d, 4)
    return jnp.where(ln.half, d, turned), jnp.where(ln.half, turned, d)


def unmix_tile(wm, t, d_ref, x_ref, de, ln):
    groups = x_ref.shape[1] // 8
    outs = wm.shape[2]

    def expand(p, _):
        rows = pl.ds(pl.multiple_of(8 * p, 8), 8)
        for s in range(2):
            vals = []
            for ri in range(2):
                m = ln.to_matrix(d_ref[t, rows, 256 * s + 128 * ri : 256 * s + 128 * ri + 128])
                vals.append(both_outputs(m, ln))
            for a in range(2):
                pats = []
                for ri in range(2):
                    m = vals[ri][a]
                    m2 = ln.swap(m, 2)
                    outer = (ln.s4 == 0) | (ln.s4 == 3)
                    pats.append((jnp.where(outer, m, m2), jnp.where(outer, m2, m)))
                for c in range(2):
                    here = pl.ds(pl.multiple_of(16 * p + 8 * a, 8), 8)
                    de[s, c, 0, here, :] = pats[0][c]
                    de[s, c, 1, here, :] = pats[1][c]
                    de[s, c, 2, here, :] = pats[0][c] + pats[1][c]
        return 0

    lax.fori_loop(0, outs // 2, expand, 0)

    def pair(p, _):
        acc = {}
        for o in range(outs):
            w = []
            for a in range(2):
                where = pl.ds(pl.multiple_of(16 * p + 8 * a, 8), 8)
                wr, wi = wm[t, 0, o, where, :], wm[t, 1, o, where, :]
                w.append((wr, wi, wr - wi))
            for s in range(2):
                for c in range(2):
                    for q in range(3):
                        d = de[s, c, q, 8 * o : 8 * o + 8, :]
                        for a in range(2):
                            key = (a, s, c, q)
                            acc[key] = w[a][q] * d + acc[key] if key in acc else w[a][q] * d
        for a in range(2):
            rows = pl.ds(pl.multiple_of(16 * p + 8 * a, 8), 8)
            for s in range(2):
                for ri in range(2):
                    red = []
                    for c in range(2):
                        t1, t2, t3 = (acc[a, s, c, q] for q in range(3))
                        value = t1 + t2 if ri == 0 else t3 - t1 + t2
                        red.append(value + ln.swap(value, 3))
                    q0, q1 = red
                    q0s, q1s = ln.swap(q0, 1), ln.swap(q1, 1)
                    f = jnp.where(ln.low, jnp.where(ln.even, q0, q0s), jnp.where(ln.even, q1s, q1))
                    h = jnp.where(ln.low, jnp.where(ln.even, q1s, q1), jnp.where(ln.even, q0, q0s))
                    x_ref[t, rows, 256 * s + 128 * ri : 256 * s + 128 * ri + 128] = 0.5 * (f + ln.sign * h)
        return 0

    lax.fori_loop(0, groups // 2, pair, 0)


def outer_expand(ln, outs, load, put):
    def one(p, _):
        for s in range(2):
            both = [both_outputs(ln.to_entries(load(p, s, ri)), ln) for ri in range(2)]
            for a in range(2):
                parts = [(both[ri][a], ln.swap(both[ri][a], 2)) for ri in range(2)]
                for r in range(2):
                    put(s, r, 0, 2 * p + a, parts[0][r])
                    put(s, r, 1, 2 * p + a, parts[1][r])
                    put(s, r, 2, 2 * p + a, parts[0][r] + parts[1][r])
        return 0

    lax.fori_loop(0, outs // 2, one, 0)


def outer_sums(devices, outs, groups, load_x, load_d, first, store, unroll):
    ob, kb = outs // 2, groups // 2

    def block(q, r, o0, k0):
        total = {}
        if first is not None:
            total = {(a, k): first(r, q, o0 + a, k0 + 8 * k) for a in range(ob) for k in range(kb)}
        for n in range(devices):
            for s in range(2):
                d = [load_d(n, s, r, q, o0 + a) for a in range(ob)]
                for k in range(kb):
                    x = load_x(n, s, q, k0 + 8 * k)
                    for a in range(ob):
                        total[a, k] = total[a, k] + d[a] * x if (a, k) in total else d[a] * x
        for (a, k), value in total.items():
            store(r, q, o0 + a, k0 + 8 * k, value)

    for q in range(3):
        if unroll:
            for r in range(2):
                for o0 in (0, ob):
                    for k0 in (0, 8 * kb):
                        block(q, r, o0, k0)
            continue

        def one(b, _):
            block(q, lax.rem(b, 2), lax.rem(lax.div(b, 2), 2) * ob, lax.div(b, 4) * (8 * kb))
            return 0

        lax.fori_loop(0, 8, one, 0)


def eight(row):
    return pl.ds(row if isinstance(row, int) else pl.multiple_of(row, 8), 8)


def outer_row(outs, rows, r, q, o, k):
    return ((r * 3 + q) * outs + o) * rows + k


def fold_point(pg, spread, rows, point, bias, scale):
    total = pg[0]
    for n in range(1, pg.shape[0]):
        total = total + pg[n]
    total = total * scale
    outs = total.shape[0] // 4
    for k in range(3):
        rows[k] = total[:, 128 * k : 128 * k + 128]
    blades = [None] * 4
    ones = jnp.ones((8, 128), jnp.bfloat16)
    for a in range(4):
        some = pl.ds(a, outs, stride=4)
        high, low = split(jnp.concatenate([rows[0, some, :], rows[1, some, :]], axis=1))
        for b in range(4):
            dot = functools.partial(lax.dot_general, dimension_numbers=NT, preferred_element_type=jnp.float32)
            value = dot(high, spread[b]) + dot(low, spread[b])
            value = -value if minus_sign(a, b) else value
            blades[a ^ b] = value if blades[a ^ b] is None else blades[a ^ b] + value
        high, low = split(rows[2, some, :])
        bias[a : a + 1, :] = (dot(ones, high) + dot(ones, low))[0:1, :]
    for c in range(4):
        point[:, c, :] = blades[c][:, : point.shape[2]]


def minus_sign(a, b):
    return b == (3 if a < 2 else 1)


def tail_kernel(scale, point_scale, steps, partial, x_ref, d_ref, pg, spread, *refs):
    part_ref, refs = (refs[0], refs[1:]) if partial else (None, refs)
    results, (g_ref, point, bias, *outs_ref), refs = refs[:4], refs[4:11], refs[11:]
    (acc, xd, de, rows3, sems), held = refs[:5], refs[5:]
    ln = Lanes()
    tile, side, step = pl.program_id(0), pl.program_id(1), pl.program_id(2)
    devices, rows = x_ref.shape[0], x_ref.shape[2]
    groups = rows // 8
    outs = d_ref.shape[2] // 4

    def load(i):
        return pltpu.make_async_copy(results[i], held[i], sems.at[0, i])

    def store(i):
        return pltpu.make_async_copy(held[i], outs_ref[i], sems.at[1, i])

    @pl.when((tile == 0) & (side == 0) & (step == 0))
    def _():
        for i in range(4):
            load(i).start()
        fold_point(pg, spread, rows3, point, bias, point_scale)

    @pl.when((tile == 1) & (side == 0) & (step == 0))
    def _():
        for i in range(4):
            load(i).wait()
            store(i).start()

    @pl.when((tile == TILES - 1) & (side == 1) & (step == steps - 1))
    def _():
        for i in range(4):
            store(i).wait()

    @pl.when((side == 0) | (steps > 1))
    def _():
        def expand(n, _):
            def put(s, r, q, o, value):
                de[n, s, r, q, o] = value

            outer_expand(
                ln, outs, lambda p, s, ri: d_ref[n, 0, eight(8 * p), 256 * s + 128 * ri : 256 * s + 128 * ri + 128], put
            )
            return 0

        lax.fori_loop(0, devices, expand, 0)

    def differ(n, _):
        for s in range(2):
            xd[n, s] = x_ref[n, 0, :, 256 * s : 256 * s + 128] - x_ref[n, 0, :, 256 * s + 128 : 256 * s + 256]
        return 0

    lax.fori_loop(0, devices, differ, 0)

    def load_x(n, s, q, row):
        if q == 2:
            return xd[n, s, eight(row), :]
        return x_ref[n, 0, eight(row), 256 * s + 128 * q : 256 * s + 128 * q + 128]

    def first(r, q, o, row):
        if partial:
            return part_ref[0, 0, eight(outer_row(outs, rows, r, q, o, row)), :]
        return jnp.where(step == 0, 0.0, acc[r, q, o, eight(row), :])

    def keep(r, q, o, row, value):
        acc[r, q, o, eight(row), :] = value

    outer_sums(
        devices,
        outs,
        groups,
        load_x,
        lambda n, s, r, q, o: de[n, s, r, q, o],
        first if partial or steps > 1 else None,
        keep,
        True,
    )

    @pl.when(step == steps - 1)
    def _():
        def finish(o, _):
            for g in range(groups):
                where = slice(8 * g, 8 * g + 8)
                for ri in range(2):
                    v = []
                    for r in range(2):
                        t1, t2 = acc[r, 0, o, where, :], acc[r, 1, o, where, :]
                        v.append(t1 + t2 if ri == 0 else acc[r, 2, o, where, :] - t1 + t2)
                    folded = jnp.where(ln.low, v[0], v[1]) + ln.swap(jnp.where(ln.low, v[1], v[0]), 3)
                    out = (folded * ln.sign + ln.swap(folded, 1)) * (0.5 * scale)
                    g_ref[ri, o, 2 * g : 2 * g + 2, :, :] = out.reshape(2, 4, 128)
            return 0

        lax.fori_loop(0, outs, finish, 0)


def tail_pass(x, d, pg, part, results, scale, point_scale):
    count, rows = x.shape[0], x.shape[2]
    own = d.shape[2]
    outs = own // 4
    group = count if count <= 8 else 8
    steps = count // group
    any_space = pl.BlockSpec(memory_space=pl.ANY)
    parts = [] if part is None else [part]
    return pl.pallas_call(
        functools.partial(tail_kernel, scale, point_scale, steps, part is not None),
        grid=(TILES, 2, steps),
        in_specs=[
            pl.BlockSpec((group, 1, rows // 2, 512), lambda t, h, n: (n, t, h, 0)),
            pl.BlockSpec((group, 1, own, 512), lambda t, h, n: (n, t, 0, 0)),
            pl.BlockSpec(pg.shape, lambda t, h, n: (0, 0, 0)),
            pl.BlockSpec((4, 128, 256), lambda t, h, n: (0, 0, 0)),
        ]
        + [pl.BlockSpec((1, 1, *p.shape[2:]), lambda t, h, n: (t, h, 0, 0)) for p in parts]
        + [any_space] * 4,
        out_specs=[
            pl.BlockSpec((2, outs, rows // 8, 4, 128), lambda t, h, n: (0, 0, h, 0, t)),
            pl.BlockSpec((outs, 4, rows // 4), lambda t, h, n: (0, 0, 0)),
            pl.BlockSpec((4, outs), lambda t, h, n: (0, 0)),
        ]
        + [any_space] * 4,
        out_shape=[
            jax.ShapeDtypeStruct((2, outs, rows // 4, 4, MODES), jnp.float32),
            jax.ShapeDtypeStruct((outs, 4, rows // 4), jnp.float32),
            jax.ShapeDtypeStruct((4, outs), jnp.float32),
        ]
        + [jax.ShapeDtypeStruct(r.shape, r.dtype) for r in results],
        scratch_shapes=[
            pltpu.VMEM((2, 3, outs, rows // 2, 128), jnp.float32),
            pltpu.VMEM((group, 2, rows // 2, 128), jnp.float32),
            pltpu.VMEM((group, 2, 2, 3, outs, 8, 128), jnp.float32),
            pltpu.VMEM((3, own, 128), jnp.float32),
            pltpu.SemaphoreType.DMA((2, 4)),
        ]
        + [pltpu.VMEM(r.shape, r.dtype) for r in results],
        compiler_params=pltpu.CompilerParams(vmem_limit_bytes=VMEM_LIMIT),
        cost_estimate=pl.CostEstimate(flops=600 << 20, bytes_accessed=46 << 20, transcendentals=0),
        name="tail_pass",
    )(x, d, pg, jnp.asarray(interleave(rows // 4)), *parts, *results)


MESH = pl.DeviceIdType.MESH


ERFC_SCALE = 0.282842712474619
ERFC = (
    0.11596259978194932,
    0.08090248108382336,
    0.23415924605220384,
    -0.1854802317493698,
    0.3545891457413051,
    -0.10013325473465298,
)


def normal_cdf(u):
    bell = jnp.exp(u * u * -0.5)
    t = 1.0 / (1.0 + ERFC_SCALE * jnp.abs(u))
    tail = ERFC[-1]
    for factor in ERFC[-2::-1]:
        tail = tail * t + factor
    tail = tail * t * bell
    return jnp.where(u >= 0.0, 1.0 - tail, tail), bell


def smem():
    return pl.BlockSpec(memory_space=pltpu.SMEM)


def vmem():
    return pl.BlockSpec(memory_space=pltpu.VMEM)


def grids():
    return ((LB, CB // 4, 0, NB), (LS, CS // 4, NB, NS))


def pieces():
    return [(s, j) for s, (_, count, _, _) in enumerate(grids()) for j in range(count)]


class Place:
    def __init__(self, count):
        self.me = lax.axis_index("chan")
        self.x = self.me // 2
        self.core = self.me % 2
        other, across = 1 - self.core, 1 - self.x
        self.peer = (2 * self.x + other, 2 * across + self.core, 2 * across + other)
        self.other_core, self.other_x = other, across
        self.count = count
        self.dp = lax.axis_index("dp")
        odd, pair = self.dp % 2, self.dp // 2
        self.pos = (1 - odd) * pair + odd * (count - 1 - pair)

    def at_pos(self, p):
        n = self.count
        p = (p + n) % n
        back = p // (n // 2)
        return (1 - back) * (2 * p) + back * (2 * (n - 1 - p) + 1)

    def copy(self, src, dst, send, recv, r):
        return pltpu.make_async_remote_copy(
            src_ref=src,
            dst_ref=dst,
            send_sem=send,
            recv_sem=recv,
            device_id={"chan": self.peer[r]},
            device_id_type=MESH,
        )

    def barrier(self):
        sem = pltpu.get_barrier_semaphore()
        for r in range(3):
            pl.semaphore_signal(sem, inc=1, device_id={"chan": self.peer[r]}, device_id_type=MESH)
        ring = ring_fits(self.count)
        for d in (1, -1) if ring else ():
            pl.semaphore_signal(sem, inc=1, device_id={"dp": self.at_pos(self.pos + d)}, device_id_type=MESH)
        pl.semaphore_wait(sem, 5 if ring else 3)


class ToCells:
    def __init__(self, here, big, small, dst, send, recv, local):
        self.here, self.srcs, self.dst, self.send, self.recv, self.local = here, (big, small), dst, send, recv, local

    def parts(self, s, j, who):
        width, count, first, cells = grids()[s]
        src = self.srcs[s].at[0, :, :, pl.ds(pl.multiple_of(cells * who + width * j, 128), width)]
        return src, self.dst.at[pl.ds(12 * self.here.me, 12), :, pl.ds(first + width * j, width)], s * grids()[0][1] + j

    def to(self, s, j, r):
        src, dst, k = self.parts(s, j, self.here.peer[r])
        return self.here.copy(src, dst, self.send.at[r, k], self.recv.at[r, k], r)

    def own(self, s, j):
        src, dst, k = self.parts(s, j, self.here.me)
        return pltpu.make_async_copy(src, dst, self.local.at[k])

    def across(self, s, j):
        for r in (1, 2):
            self.to(s, j, r).start()

    def near(self, s, j):
        self.to(s, j, 0).start()
        self.own(s, j).start()

    def arrived(self, s, j):
        self.own(s, j).wait()
        for r in range(3):
            self.to(s, j, r).wait_recv()

    def sent(self, s, j):
        for r in range(3):
            self.to(s, j, r).wait_send()


class ToChannels:
    def __init__(self, here, src, big, small, send, recv, local):
        self.here, self.src, self.dsts, self.send, self.recv, self.local = here, src, (big, small), send, recv, local

    def parts(self, s, j, who):
        width, count, first, cells = grids()[s]
        src = self.src.at[pl.ds(12 * who, 12), :, pl.ds(first + width * j, width)]
        lanes = pl.ds(pl.multiple_of(cells * self.here.me + width * j, 128), width)
        return src, self.dsts[s].at[0, :, :, lanes], s * grids()[0][1] + j

    def to(self, s, j, r):
        src, dst, k = self.parts(s, j, self.here.peer[r])
        return self.here.copy(src, dst, self.send.at[r, k], self.recv.at[r, k], r)

    def own(self, s, j):
        src, dst, k = self.parts(s, j, self.here.me)
        return pltpu.make_async_copy(src, dst, self.local.at[k])

    def start(self, s, j):
        for r in (1, 2, 0):
            self.to(s, j, r).start()
        self.own(s, j).start()


class Gather:
    def __init__(self, here, ref, send, recv, own):
        self.here, self.ref, self.send, self.recv, self.own = here, ref, send, recv, own

    def rows(self, t, who):
        return self.ref.at[t, pl.ds(pl.multiple_of(self.own * who, 8), self.own), :]

    def direct(self, t, r):
        block = self.rows(t, self.here.me)
        return self.here.copy(block, block, self.send.at[r, t], self.recv.at[r, t], r)

    def onward(self, t):
        block = self.rows(t, self.here.peer[1])
        return self.here.copy(block, block, self.send.at[2, t], self.recv.at[2, t], 0)

    def start(self, t):
        self.direct(t, 1).start()
        self.direct(t, 0).start()

    def forward(self, t):
        self.direct(t, 1).wait_recv()
        self.onward(t).start()

    def arrived(self, t):
        self.direct(t, 0).wait_recv()
        self.onward(t).wait_recv()

    def sent(self, t):
        self.direct(t, 0).wait_send()
        self.direct(t, 1).wait_send()
        self.onward(t).wait_send()


class SumAll:
    def __init__(self, here, part, first, second, total, send, recv, ln):
        self.here, self.part, self.first, self.second, self.total = here, part, first, second, total
        self.send, self.recv, self.ln = send, recv, ln
        self.half = part.shape[1] // 2

    def rows(self, core):
        return pl.ds(pl.multiple_of(self.half * core, 8), self.half)

    def step(self, k, s, t):
        lanes = pl.ds(256 * s, 256)
        sems = self.send.at[k, s, t], self.recv.at[k, s, t]
        if k == 0:
            src, dst = self.part.at[t, self.rows(self.here.other_core), lanes], self.first.at[t, :, lanes]
            return self.here.copy(src, dst, *sems, 0)
        if k == 1:
            return self.here.copy(self.first.at[t, :, lanes], self.second.at[t, :, lanes], *sems, 1)
        block = self.total.at[t, self.rows(self.here.core), lanes]
        return self.here.copy(block, block, *sems, 0)

    def across(self, s, t):
        self.step(0, s, t).wait()
        lanes = slice(256 * s, 256 * s + 256)
        self.first[t, :, lanes] = self.first[t, :, lanes] + self.part[t, self.rows(self.here.core), lanes]
        self.step(1, s, t).start()

    def back(self, s, t):
        self.step(1, s, t).wait_recv()
        ln = self.ln

        def group(g, _):
            rows = pl.ds(pl.multiple_of(8 * g, 8), 8)
            mine = pl.ds(pl.multiple_of(self.half * self.here.core + 8 * g, 8), 8)
            for ri in range(2):
                lanes = slice(256 * s + 128 * ri, 256 * s + 128 * ri + 128)
                self.total[t, mine, lanes] = ln.to_entries(self.first[t, rows, lanes] + self.second[t, rows, lanes])
            return 0

        lax.fori_loop(0, self.half // 8, group, 0)
        self.step(2, s, t).start()


class SumScatter:
    def __init__(self, here, part, first, second, result, send, recv, lead, width):
        self.here, self.part, self.first, self.second, self.result = here, part, first, second, result
        self.send, self.recv, self.lead, self.width = send, recv, lead, width
        self.own = result.shape[-2]

    def rows(self, ref, t, s, block):
        where = (pl.ds(pl.multiple_of(self.own * block, 8), self.own), pl.ds(self.width * s, self.width))
        return ref.at[(t, *where)] if self.lead else ref.at[where]

    def over(self, s, t, x):
        src = self.rows(self.part, t, s, 2 * x + self.here.other_core)
        return self.here.copy(src, self.rows(self.first, t, s, x), self.send.at[x, s, t], self.recv.at[x, s, t], 0)

    def across_copy(self, s, t):
        src, dst = self.rows(self.first, t, s, self.here.other_x), self.rows(self.second, t, s, 0)
        return self.here.copy(src, dst, self.send.at[2, s, t], self.recv.at[2, s, t], 1)

    def start(self, s, t):
        for x in range(2):
            self.over(s, t, x).start()

    def across(self, s, t):
        for x in range(2):
            self.over(s, t, x).wait_recv()
            slot = self.rows(self.first, t, s, x)
            slot[...] = slot[...] + self.rows(self.part, t, s, 2 * x + self.here.core)[...]
        self.across_copy(s, t).start()

    def finish(self, s, t):
        self.across_copy(s, t).wait_recv()
        result = self.rows(self.result, t, s, 0)
        result[...] = self.rows(self.first, t, s, self.here.x)[...] + self.rows(self.second, t, s, 0)[...]

    def sent(self, s, t):
        for x in range(2):
            self.over(s, t, x).wait_send()
        self.across_copy(s, t).wait_send()


class Ring:
    def __init__(self, here, streams, send, recv):
        self.here, self.streams, self.send, self.recv = here, streams, send, recv
        self.steps = here.count // 2 if ring_fits(here.count) else 0

    def origin(self, way, step):
        return self.here.at_pos(self.here.pos - (step + 1) * (1 - 2 * way))

    def part(self, way, step):
        return way if step == self.steps - 1 else None

    def copies(self, way, step):
        target = self.here.at_pos(self.here.pos + (1 - 2 * way))
        part = self.part(way, step)
        out = []
        for k, place in self.streams:
            out.append(
                pltpu.make_async_remote_copy(
                    src_ref=place(way, step - 1, part),
                    dst_ref=place(way, step, part),
                    send_sem=self.send.at[k, way, step],
                    recv_sem=self.recv.at[k, way, step],
                    device_id={"dp": target},
                    device_id_type=MESH,
                )
            )
        return out

    def start(self, step):
        for way in range(2):
            for cp in self.copies(way, step) if step < self.steps else ():
                cp.start()

    def advance(self, step, then):
        for way in range(2) if step <= self.steps else ():
            for cp in self.copies(way, step - 1):
                cp.wait_recv()
            for cp in self.copies(way, step) if step < self.steps else ():
                cp.start()
            for cp in then(way, step - 1):
                cp.start()

    def first_sent(self):
        for way in range(2) if self.steps else ():
            for cp in self.copies(way, 0):
                cp.wait_send()

    def finish(self, then, first=0, kept=0):
        for way in range(2):
            for step in range(self.steps):
                for cp in self.copies(way, step) if step >= first else ():
                    cp.wait_send()
                for cp in then(way, step) if step >= kept else ():
                    cp.wait()


def ring_fits(count):
    return count == 8


def spectral_piece(z_ref, zh, zl, yh, yl, pre, inverse, phase, chunk, count, s, rows, width):
    vth, vtl, wth, wtl = inverse
    for j in range(count):
        turn_modes(z_ref, zh, zl, phase, chunk + j, s, rows, rows * j)
    used = slice(0, count * rows)
    first_stage(zh[used, :], zl[used, :], vth, vtl, yh, yl, used)

    def tile(n, _):
        lanes = pl.ds(pl.multiple_of(256 * n, 256), 256)
        pre[used, lanes] = dot3(yh[used, :], yl[used, :], wth[:, lanes], wtl[:, lanes])
        return 0

    lax.fori_loop(0, width // 256, tile, 0)


def main_kernel(
    dp_count, live_big, live_small, bias_in, weights, spread, big, small, w, cbig, csmall, tables_in, phases,
    big_out, small_out, big_grad, small_grad, pg_all, gathered,
    tabs, vbuf, cbuf, ob, osm, gb, gs, kh, kl, sh, sl, x1, z1, x2, x2a, x2b, x2t, dza, dzb, dzo, dxo, xs, pgs,
    wm, xe, de, hid, zh, zl, yh, yl, pre, blades, c_own, c_all, square, ch, cl, dh, dl, pg, pga, pgb, pgo,
    load_sem, own_sem, half_sem, chalf_sem, w_sem, local_sem, out_sem, ctd_half_sem,
    v_send, v_recv, c_send, c_recv, o_send, o_recv, d_send, d_recv, p_send, p_recv,
    x1_send, x1_recv, z1_send, z1_recv, z2_send, z2_recv, x2_send, x2_recv,
    dz_send, dz_recv, dx_send, dx_recv, pg_send, pg_recv,
    xr_send, xr_recv, xc_send, xc_recv, dr_send, dr_recv, keep_sem, ready, near_sem, sums_sem,
):
    here = Place(dp_count)
    ln = Lanes()
    pbi, psi, pbo, pso = phases
    rows = x1.shape[1]
    own = rows // 4
    outs = own // 4
    groups = rows // 8
    forward = (tabs[0:4], tabs[4:8])
    inverse = (tabs[8:12], tabs[12:16])
    phase_in, phase_out = (pbi, psi), (pbo, pso)
    own_rows = pl.ds(pl.multiple_of(own * here.me, 8), own)
    loads = [pltpu.make_async_copy(src, dst, load_sem.at[i]) for i, (src, dst) in enumerate(zip(tables_in, tabs))]
    g_planes = [pltpu.make_async_copy(cbig, gb, own_sem.at[2]), pltpu.make_async_copy(csmall, gs, own_sem.at[3])]
    planes = [pltpu.make_async_copy(big, ob, own_sem.at[0]), pltpu.make_async_copy(small, osm, own_sem.at[1])]

    def w_copy(t):
        dst = wm.at[t].reshape(2, outs, rows // 4, 4, 128)
        return pltpu.make_async_copy(w.at[:, :, :, :, pl.ds(128 * t, 128)], dst, w_sem.at[t])

    def point_copy(r):
        return here.copy(c_own, c_all.at[own_rows, :], p_send.at[r], p_recv.at[r], r)

    live = (live_big[0].astype(jnp.float32), live_small[0].astype(jnp.float32))

    fields = ToCells(here, ob, osm, vbuf, v_send, v_recv, half_sem)
    grads = ToCells(here, gb, gs, cbuf, c_send, c_recv, chalf_sem)
    outputs = ToChannels(here, vbuf, big_out, small_out, o_send, o_recv, out_sem)
    backs = ToChannels(here, cbuf, ob, osm, d_send, d_recv, ctd_half_sem)
    x1_gather = Gather(here, x1, x1_send, x1_recv, own)
    z1_gather = Gather(here, z1, z1_send, z1_recv, own)
    z2 = x2
    z2_gather = Gather(here, z2, z2_send, z2_recv, own)
    x2_sum = SumAll(here, x2, x2a, x2b, x2t, x2_send, x2_recv, ln)
    dz_sum = SumScatter(here, x1, dza, dzb, dzo, dz_send, dz_recv, True, 256)
    dx_sum = SumScatter(here, z1, x2a, x2b, dxo, dx_send, dx_recv, True, 512)
    pg_sum = SumScatter(here, pg, pga, pgb, pgo, pg_send, pg_recv, False, PG)
    half_rows = pl.ds(pl.multiple_of(2 * own * here.core, 8), 2 * own)
    lanes_of = (pl.ds(0, 256), pl.ds(256, 256))

    last = dp_count // 2 - 1
    ring = ring_fits(dp_count)
    x2_near, x2_far, dz_far, sums_out = gathered if ring else (None,) * 4

    def far(way, k):
        return 2 if k == last else way

    def span(first, size, part):
        if part is None:
            return pl.ds(first, size)
        return pl.ds(first + part * (size // 2), size // 2)

    def half_span(part):
        size = 2 * own if part is None else own
        first = 2 * own * here.core + (0 if part is None else own * part)
        return pl.ds(pl.multiple_of(first, 8), size)

    def x2_place(s):
        def place(way, k, part):
            if k < 0:
                return x2t.at[:, half_span(part), lanes_of[s]]
            slot = k if k == last else 4 * way + k
            return xs.at[slot, :, span(0, 2 * own, part), lanes_of[s]]

        return place

    def dz_place(s):
        def place(way, k, part):
            if k < 0:
                return dzo.at[:, span(0, own, part), lanes_of[s]]
            ref = x2t if way == 0 or k == last else z2
            return ref.at[:, span(own * k, own, part), lanes_of[s]]

        return place

    def pg_place(way, k, part):
        if k < 0:
            return pgo.at[span(0, own, part), :]
        return pgs.at[k if k == last else 4 * way + k, span(0, own, part), :]

    x2_rings = [Ring(here, [(s, x2_place(s))], xr_send, xr_recv) for s in range(2)]
    dz_rings = [
        Ring(here, [(0, dz_place(0))], dr_send, dr_recv),
        Ring(here, [(1, dz_place(1)), (2, pg_place)], dr_send, dr_recv),
    ]

    def keep_x2(s):
        def keep(way, k):
            part = x2_rings[s].part(way, k)
            slot = x2_place(s)(way, k, part)
            ref = x2_near.at[1 + 2 * k + way] if k < 2 else x2_far.at[far(way, k)]
            block = ref.at[:, half_span(part), lanes_of[s]]
            return (
                here.copy(slot, block, xc_send.at[s, way, k], xc_recv.at[s, way, k], 0),
                pltpu.make_async_copy(slot, block, keep_sem.at[s, way, k]),
            )

        return keep

    def keep_dz(s):
        def keep(way, k):
            ring = dz_rings[s]
            i, part = ring.origin(way, k), ring.part(way, k)
            out = []
            if k > 1:
                block = dz_far.at[far(way, k), :, span(0, own, part), lanes_of[s]]
                out.append(pltpu.make_async_copy(dz_place(s)(way, k, part), block, keep_sem.at[2 + s, way, k]))
            if s == 1:
                block = pg_all.at[i, span(0, own, part), :]
                out.append(pltpu.make_async_copy(pg_place(way, k, part), block, keep_sem.at[4, way, k]))
            return out

        return keep

    def x2_done():
        for s in range(2):
            for way in range(2):
                for k in range(2):
                    for cp in keep_x2(s)(way, k):
                        cp.wait()

    def x2_advance(s, step):
        x2_rings[s].advance(step, keep_x2(s))

    def dz_advance(s, step):
        dz_rings[s].advance(step, keep_dz(s))

    def tell_ready(s):
        if ring_fits(dp_count):
            x2_rings[s].first_sent()
            for way in range(2):
                target = here.at_pos(here.pos + (1 - 2 * way))
                pl.semaphore_signal(ready.at[s], inc=1, device_id={"dp": target}, device_id_type=MESH)

    def dz_start(s):
        if ring_fits(dp_count):
            pl.semaphore_wait(ready.at[s], 2)
            dz_rings[s].start(0)

    for cp in planes + loads[:8]:
        cp.start()
    here.barrier()
    for cp in planes:
        cp.wait()
    for j in range(CS // 4):
        fields.across(1, j)
    for s, j in pieces():
        fields.near(s, j)
    for t in range(TILES):
        w_copy(t).start()
    for cp in loads[8:] + g_planes:
        cp.start()
    for cp in loads[:8]:
        cp.wait()

    for ref, h, l, count, width in ((ob, kh, kl, CB, LB), (osm, sh, sl, CS, LS)):

        def stack(c, _):
            high, low = split(ref[0, :, :, pl.ds(pl.multiple_of(width * c, 128), width)].reshape(own, width))
            where = pl.ds(pl.multiple_of(own * c, 16), own)
            h[where, :] = high
            l[where, :] = low
            return 0

        lax.fori_loop(0, count, stack, 0)

    def own_modes(s):
        h, l, phase, count = ((kh, kl, pbi, CB), (sh, sl, psi, CS))[s]
        wh, wl, vh, vl = forward[s]
        first_stage(h[...], l[...], wh, wl, yh, yl, slice(0, count * own))

        def own_tile(t, _):
            re, im = forward_tile(yh, yl, vh, vl, phase, 0, count, own, t)
            x1[t, own_rows, 256 * s : 256 * s + 128] = re
            x1[t, own_rows, 256 * s + 128 : 256 * s + 256] = im
            if s == 0:
                x1_gather.start(t)
            return 0

        lax.fori_loop(0, TILES, own_tile, 0)

    own_modes(1)
    own_modes(0)
    fields.across(0, 0)
    blades[...] = jnp.zeros_like(blades)
    blades[0, :, : rows // 4] = weights[...].reshape(own, rows // 4)
    dense = jnp.zeros((own, 256), jnp.float32)
    for b in range(4):
        for g in range(own // 8):
            value = blades[0, 8 * g : 8 * g + 8, :]
            value = ln.swap(value, b) if b else value
            minus = (ln.s4 < 2) if b == 3 else (ln.s4 >= 2) if b == 1 else None
            blades[1, 8 * g : 8 * g + 8, :] = value if minus is None else jnp.where(minus, -value, value)
        high, low = split(blades[1])
        dense += jnp.dot(high, spread[b], preferred_element_type=jnp.float32)
        dense += jnp.dot(low, spread[b], preferred_element_type=jnp.float32)
    c_own[:, :256] = dense
    row = lax.broadcasted_iota(jnp.int32, (own, PG - 256), 0)
    column = jnp.zeros((own, PG - 256), jnp.float32)
    for o in range(outs):
        for a in range(4):
            column = jnp.where(row == 4 * o + a, bias_in[a, o], column)
    c_own[:, 256:] = column
    c_all[own_rows, :] = c_own[...]
    for r in range(3):
        point_copy(r).start()

    for t in range(TILES):
        w_copy(t).wait()

        def convert(i, _):
            ri, o = lax.rem(i, 2), lax.div(i, 2)
            for g in range(groups):
                where = slice(8 * g, 8 * g + 8)
                wm[t, ri, o, where, :] = ln.to_matrix(wm[t, ri, o, where, :])
            return 0

        lax.fori_loop(0, 2 * outs, convert, 0)
        x1_gather.forward(t)

    def mix_first(t, _):
        x1_gather.arrived(t)
        mix_tile(wm, t, lambda where, lanes: ln.to_entries(x1[t, where, lanes]), z1, here.me, xe, ln)
        z1_gather.start(t)

        @pl.when(t >= 1)
        def _():
            z1_gather.forward(t - 1)

        return 0

    lax.fori_loop(0, TILES, mix_first, 0)
    for cp in g_planes:
        cp.wait()
    z1_gather.forward(TILES - 1)
    fields.across(0, 1)
    fields.across(0, 2)
    grads.across(0, 0)
    for s, j in pieces():
        grads.near(s, j)
    for r in range(3):
        point_copy(r).wait_recv()
    square[0:rows, :] = c_all[:, :256]
    square[rows:256, :] = jnp.zeros((256 - rows, 256), jnp.float32)
    ch[...], cl[...] = split(c_all[:, :rows])
    dh[...], dl[...] = split(jnp.transpose(square[...])[:rows, :rows])

    for cp in loads[8:]:
        cp.wait()

    def pointwise(s, j, load, store):
        width, count, first, cells_here = grids()[s]

        def cells(n, _):
            lanes = pl.ds(pl.multiple_of(first + j * width + 256 * n, 256), 256)
            vh, vl = split(load(lanes))
            store(lanes, dot3(ch[...], cl[...], vh, vl) + c_all[:, 256:257])
            return 0

        lax.fori_loop(0, width // 256, cells, 0)

    def load_field(lanes):
        return vbuf[:, :, lanes].reshape(rows, 256)

    def store_field(lanes, value):
        vbuf[:, :, lanes] = value.reshape(rows // 4, 4, 256)

    def load_hid(lanes):
        return hid[:, lanes]

    def store_hid(lanes, value):
        hid[:, lanes] = value

    def point_piece(s, j):
        fields.arrived(s, j)
        pointwise(s, j, load_field, store_hid)

    for j in range(CS // 4):
        point_piece(1, j)
    point_piece(0, 0)

    def z1_arrived(t, _):
        z1_gather.arrived(t)
        return 0

    lax.fori_loop(0, TILES, z1_arrived, 0)

    def each_tile(fn):
        def one(t, _):
            fn(t)
            return 0

        lax.fori_loop(0, TILES, one, 0)

    for s, (width, count, first, cells_here) in enumerate(grids()):
        wh, wl, vh, vl = forward[s]
        chunk = here.me * count
        spectral_piece(z1, zh, zl, yh, yl, pre, inverse[s], phase_out[s], chunk, count, s, rows, width)
        if s == 1:
            each_tile(lambda t: x2_sum.across(0, t))
        for j in range(count):
            if s == 0 and j > 0:
                point_piece(0, j)

            def cells(n, _):
                at = pl.ds(pl.multiple_of(256 * n, 256), 256)
                lanes = pl.ds(pl.multiple_of(first + j * width + 256 * n, 256), 256)
                u = pre[rows * j : rows * (j + 1), at] + hid[:, lanes]
                out = load_field(lanes) + u * normal_cdf(u)[0]
                hid[:, lanes] = out
                oh, ol = split(out)
                kh[rows * j : rows * (j + 1), at] = oh
                kl[rows * j : rows * (j + 1), at] = ol
                return 0

            lax.fori_loop(0, width // 256, cells, 0)
        if s == 1:
            each_tile(lambda t: x2_sum.back(0, t))
            x2_rings[0].start(0)

        used = slice(0, count * rows)
        first_stage(kh[used, :width], kl[used, :width], wh, wl, yh, yl, used)

        def modes(t, _):
            re, im = forward_tile(yh, yl, vh, vl, phase_in[s], chunk, count, rows, t)
            x2[t, :, 256 * s : 256 * s + 128] = re
            x2[t, :, 256 * s + 128 : 256 * s + 256] = im
            x2_sum.step(0, s, t).start()
            return 0

        lax.fori_loop(0, TILES, modes, 0)
    for s, j in pieces():
        fields.sent(s, j)
    each_tile(lambda t: x2_sum.across(1, t))
    each_tile(lambda t: x2_sum.back(1, t))
    x2_rings[1].start(0)

    def crossed(t):
        for s in range(2):
            x2_sum.step(1, s, t).wait_send()

    each_tile(crossed)

    def mix_second(t, _):
        for s in range(2):
            x2_sum.step(2, s, t).wait_recv()
        mix_tile(wm, t, lambda where, lanes: x2t[t, where, lanes], z2, here.me, xe, ln)
        z2_gather.start(t)

        @pl.when(t >= 1)
        def _():
            z2_gather.forward(t - 1)

        return 0

    lax.fori_loop(0, TILES // 2, mix_second, 0)
    x2_advance(0, 1)
    lax.fori_loop(TILES // 2, TILES, mix_second, 0)
    x2_local = pltpu.make_async_copy(x2t, x2_near.at[0] if ring else gathered[0], local_sem.at[0])
    x2_local.start()
    z2_gather.forward(TILES - 1)
    grads.across(0, 1)
    grads.across(0, 2)
    for j in range(CS // 4):
        grads.across(1, j)
    for s, j in pieces():
        pointwise(s, j, load_hid, store_field)
    x2_advance(1, 1)
    each_tile(z2_gather.arrived)
    x2_advance(0, 2)
    each_tile(x1_gather.sent)
    each_tile(z1_gather.sent)
    pg[...] = jnp.zeros_like(pg)

    for s, (width, count, first, cells_here) in enumerate(grids()):
        wh, wl, vh, vl = forward[s]
        chunk = here.me * count
        spectral_piece(z2, zh, zl, yh, yl, pre, inverse[s], phase_out[s], chunk, count, s, rows, width)
        if s == 0:
            x2_local.wait()
            each_tile(z2_gather.sent)
        each_tile(lambda t: x2_sum.step(2, s, t).wait_send())
        tell_ready(s)
        if s == 1:
            each_tile(lambda t: dz_sum.across(0, t))
            backs.start(0, 0)
        for j in range(count):
            grads.arrived(s, j)

            def cells(n, _):
                at = pl.ds(pl.multiple_of(256 * n, 256), 256)
                lanes = pl.ds(pl.multiple_of(first + j * width + 256 * n, 256), 256)
                value = hid[:, lanes]
                vh, vl = split(value)
                u = pre[rows * j : rows * (j + 1), at] + load_field(lanes)
                cdf, bell = normal_cdf(u)
                store_field(lanes, value + u * cdf)
                slope = cdf + u * (bell * (1.0 / math.sqrt(2.0 * math.pi)))
                grad = cbuf[:, :, lanes].reshape(rows, 256) * live[s] * slope
                gh, gl = split(grad)
                kh[rows * j : rows * (j + 1), at] = gh
                kl[rows * j : rows * (j + 1), at] = gl
                cbuf[:, :, lanes] = dot3(dh[...], dl[...], gh, gl).reshape(rows // 4, 4, 256)
                pg[:, :rows] += dot3(gh, gl, vh, vl, NT)
                pg[:, 256:] += grad[:, :128] + grad[:, 128:]
                return 0

            lax.fori_loop(0, width // 256, cells, 0)
            if (s, j) == (0, 1):
                x2_advance(1, 2)
        if s == 1:
            each_tile(lambda t: dz_sum.finish(0, t))
            dz_start(0)

        used = slice(0, count * rows)
        first_stage(kh[used, :width], kl[used, :width], wh, wl, yh, yl, used)

        def modes(t, _):
            re, im = forward_tile(yh, yl, vh, vl, phase_out[s], chunk, count, rows, t)
            x1[t, :, 256 * s : 256 * s + 128] = re
            x1[t, :, 256 * s + 128 : 256 * s + 256] = im
            dz_sum.start(s, t)
            return 0

        lax.fori_loop(0, TILES, modes, 0)
        x2_advance(s, 3)
    pg_sum.start(0, 0)
    each_tile(lambda t: dz_sum.across(1, t))
    pg_sum.across(0, 0)
    backs.start(0, 1)
    backs.start(0, 2)
    for j in range(CS // 4):
        backs.start(1, j)
    each_tile(lambda t: dz_sum.finish(1, t))
    pg_sum.finish(0, 0)
    dz_start(1)
    dz_local = [pltpu.make_async_copy(pgo, pg_all.at[here.dp] if ring else pg_all, local_sem.at[2])]
    if not ring:
        dz_local.append(pltpu.make_async_copy(dzo, gathered[1], local_sem.at[1]))
    for cp in dz_local:
        cp.start()

    for t in range(TILES):
        unmix_tile(wm, t, dzo, z1, xe, ln)
        dx_sum.start(0, t)
        if t >= 1:
            dx_sum.across(0, t - 1)
        if t == 1:
            dz_advance(0, 1)
    dx_sum.across(0, TILES - 1)
    for s, j in pieces():
        outputs.start(s, j)
    dz_advance(1, 1)
    dz_advance(0, 2)

    flat = wm.reshape(TILES * 2 * outs * rows, 128)
    half = rows // 2
    acc_rows = 6 * outs * half
    xd_row0 = 2 * acc_rows

    def x_near(i):
        t, h = lax.div(i, 2), lax.rem(i, 2)
        out = []
        for n in range(NEAR):
            src = x2_near.at[n, t, pl.ds(pl.multiple_of(half * h, 8), half), :]
            dst = hid.at[pl.ds(pl.multiple_of(half * h, 8), half), pl.ds(512 * n, 512)]
            out.append(pltpu.make_async_copy(src, dst, near_sem.at[h, n]))
        return out

    def sums_copy(i):
        t, h = lax.div(i, 2), lax.rem(i, 2)
        src = flat.at[pl.ds(pl.multiple_of(acc_rows * h, 8), acc_rows), :]
        return pltpu.make_async_copy(src, sums_out.at[t, h], sums_sem.at[h])

    def de_at(n, s, r, q, o):
        return eight(((((n * 2 + s) * 2 + r) * 3 + q) * outs + o) * 8)

    def near_step(i, _):
        t, h = lax.div(i, 2), lax.rem(i, 2)
        for cp in x_near(i):
            cp.wait()

        @pl.when(i + 1 < 2 * TILES)
        def _():
            for cp in x_near(i + 1):
                cp.start()

        @pl.when(i >= 2)
        def _():
            sums_copy(i - 2).wait()

        @pl.when(h == 0)
        def _():
            for n, (ref, row0) in enumerate(((dzo, 0), (x2t, 0), (z2, 0), (x2t, own), (z2, own))):

                def put(s, r, q, o, value):
                    de[de_at(n, s, r, q, o), :] = value

                outer_expand(
                    ln, outs, lambda p, s, ri: ref[t, eight(row0 + 8 * p), 256 * s + 128 * ri : 256 * s + 128 * ri + 128], put
                )

        def x_row(row):
            return eight(h * half + row)

        def differ(g, _):
            for n in range(NEAR):
                for s in range(2):
                    x = hid[x_row(8 * g), 512 * n + 256 * s : 512 * n + 256 * s + 256]
                    flat[eight(xd_row0 + (n * 2 + s) * half + 8 * g), :] = x[:, :128] - x[:, 128:]
            return 0

        lax.fori_loop(0, half // 8, differ, 0)

        def load_x(n, s, q, row):
            if q == 2:
                return flat[eight(xd_row0 + (n * 2 + s) * half + row), :]
            lane = 512 * n + 256 * s + 128 * q
            return hid[x_row(row), lane : lane + 128]

        def keep_sum(r, q, o, row, value):
            flat[eight(acc_rows * h + outer_row(outs, half, r, q, o, row)), :] = value

        outer_sums(
            NEAR, outs, half // 8, load_x, lambda n, s, r, q, o: de[de_at(n, s, r, q, o), :], None, keep_sum, False
        )
        sums_copy(i).start()
        return 0

    def near_products(lo, hi):
        if ring:
            lax.fori_loop(lo, hi, near_step, 0)

    if ring:
        x2_done()
        for cp in x_near(0):
            cp.start()
        dz_advance(1, 2)
    near_products(0, 2)
    dz_advance(0, 3)
    near_products(2, 4)
    each_tile(lambda t: dx_sum.finish(0, t))
    dz_advance(1, 3)

    for s, (g, o, dst, phase, count, width) in enumerate(
        ((gb, ob, big_grad, pbi, CB, LB), (gs, osm, small_grad, psi, CS, LS))
    ):
        vth, vtl, wth, wtl = inverse[s]
        for j in range(count):
            turn_modes(dxo, zh, zl, phase, j, s, own, own * j)
        for j in range(count // 4):
            backs.own(s, j).wait()
            for r in range(3):
                backs.to(s, j, r).wait_recv()
        used = slice(0, count * own)
        first_stage(zh[used, :], zl[used, :], vth, vtl, yh, yl, used)

        def tile(n, _):
            lanes = pl.ds(pl.multiple_of(256 * n, 256), 256)
            part = dot3(yh[used, :], yl[used, :], wth[:, lanes], wtl[:, lanes])
            for j in range(count):
                where = pl.ds(pl.multiple_of(width * j + 256 * n, 256), 256)
                o[0, :, :, where] = (
                    part[own * j : own * (j + 1)].reshape(outs, 4, 256) + g[0, :, :, where] * live[s] + o[0, :, :, where]
                )
            return 0

        lax.fori_loop(0, width // 256, tile, 0)
        if s == 0:
            near_products(4, 6)
        pltpu.make_async_copy(o, dst, local_sem.at[3 + s]).start()
    near_products(6, 8)
    for s in range(2):
        x2_advance(s, 4)
        dz_advance(s, 4)

    for cp in dz_local:
        cp.wait()
    pltpu.make_async_copy(ob, big_grad, local_sem.at[3]).wait()
    pltpu.make_async_copy(osm, small_grad, local_sem.at[4]).wait()
    for r in range(3):
        point_copy(r).wait_send()
    for s, j in pieces():
        grads.sent(s, j)
        for r in range(3):
            backs.to(s, j, r).wait_send()
        outputs.own(s, j).wait()
        for r in range(3):
            outputs.to(s, j, r).wait()

    def last_tile(t, _):
        for s in range(2):
            dz_sum.sent(s, t)
        dx_sum.sent(0, t)
        return 0

    lax.fori_loop(0, TILES, last_tile, 0)
    pg_sum.sent(0, 0)
    for i in range(2 * TILES - 2, 2 * TILES) if ring else ():
        sums_copy(i).wait()
    for s in range(2):
        x2_rings[s].finish(keep_x2(s), 1, 2)
        dz_rings[s].finish(keep_dz(s))


def main_pass(dp, live_big, live_small, bias, weights, big, small, w, cbig, csmall, tabs):
    rows = w.shape[2] * 4
    outs = w.shape[1]
    own = rows // 4
    any_space = pl.BlockSpec(memory_space=pl.ANY)
    table = tabs["table"]
    phases = (tabs["pb_in"], tabs["ps_in"], tabs["pb_out"], tabs["ps_out"])
    f32, bf16 = jnp.float32, jnp.bfloat16

    def buf(*shape, dtype=f32):
        return pltpu.VMEM(shape, dtype)

    def dma(*shape):
        return pltpu.SemaphoreType.DMA(shape)

    modes = (TILES, rows, 512)
    half, quarter = (TILES, rows // 2, 512), (TILES, own, 512)
    ring = ring_fits(dp)
    steps = max(1, dp // 2) if ring else 1
    slots = 7 if ring else 1
    lead = (dp,) if ring else ()
    if ring:
        shapes = ((NEAR, *modes), (dp - NEAR, *modes), (dp - NEAR, *quarter), (TILES, 2, 3 * outs * rows, 128))
    else:
        shapes = (modes, quarter)
    gathered = tuple(jax.ShapeDtypeStruct(shape, f32) for shape in shapes)
    chunks = (CB + CS) // 4
    return pl.pallas_call(
        functools.partial(main_kernel, dp),
        in_specs=[smem()] * 3 + [vmem()] * 2 + [any_space] * 5 + [(any_space,) * len(table), (vmem(),) * 4],
        out_specs=[any_space] * 5 + [tuple(any_space for _ in gathered)],
        out_shape=[
            jax.ShapeDtypeStruct(big.shape, f32),
            jax.ShapeDtypeStruct(small.shape, f32),
            jax.ShapeDtypeStruct(big.shape, f32),
            jax.ShapeDtypeStruct(small.shape, f32),
            jax.ShapeDtypeStruct((*lead, own, PG), f32),
            gathered,
        ],
        scratch_shapes=[
            tuple(pltpu.VMEM(a.shape, bf16) for a in table),
            buf(rows // 4, 4, NQ),
            buf(rows // 4, 4, NQ),
            buf(*big.shape),
            buf(*small.shape),
            buf(*big.shape),
            buf(*small.shape),
            buf(own * CB, LB, dtype=bf16),
            buf(own * CB, LB, dtype=bf16),
            buf(own * CS, LS, dtype=bf16),
            buf(own * CS, LS, dtype=bf16),
            buf(*modes),
            buf(*modes),
            buf(*modes),
            buf(*half),
            buf(*half),
            buf(*modes),
            buf(*half),
            buf(*quarter),
            buf(*quarter),
            buf(*quarter),
            buf(slots, *half),
            buf(slots, own, PG),
            buf(TILES, 2, outs, rows, 128),
            buf(2, 2, 3, rows, 128),
            buf(NEAR * 12 * outs * 8 if ring else 8, 128),
            buf(rows, NQ),
            buf(own * CB, 2 * MODES, dtype=bf16),
            buf(own * CB, 2 * MODES, dtype=bf16),
            buf(own * CB, 256, dtype=bf16),
            buf(own * CB, 256, dtype=bf16),
            buf(own * CB, LB),
            buf(2, own, 128),
            buf(own, PG),
            buf(rows, PG),
            buf(256, 256),
            buf(rows, rows, dtype=bf16),
            buf(rows, rows, dtype=bf16),
            buf(rows, rows, dtype=bf16),
            buf(rows, rows, dtype=bf16),
            buf(rows, PG),
            buf(2 * own, PG),
            buf(own, PG),
            buf(own, PG),
            dma(len(table)),
            dma(4),
            dma(chunks),
            dma(chunks),
            dma(TILES),
            dma(5),
            dma(chunks),
            dma(chunks),
        ]
        + [dma(3, chunks)] * 8
        + [dma(3)] * 2
        + [dma(3, TILES)] * 6
        + [dma(3, 2, TILES)] * 2
        + [dma(3, 2, TILES)] * 2
        + [dma(3, 1, TILES)] * 2
        + [dma(3, 1, 1)] * 2
        + [dma(2, 2, steps)] * 4
        + [dma(3, 2, steps)] * 2
        + [dma(5, 2, steps), pltpu.SemaphoreType.REGULAR((2,)), dma(2, NEAR), dma(2)],
        compiler_params=pltpu.CompilerParams(vmem_limit_bytes=VMEM_LIMIT, collective_id=0, has_side_effects=True),
        cost_estimate=pl.CostEstimate(flops=40 << 30, bytes_accessed=60 << 20, transcendentals=0),
        name="main_pass",
    )(live_big, live_small, bias, weights, jnp.asarray(interleave(rows // 4)), big, small, w, cbig, csmall, table, phases)


def tables():
    tabs = {}
    forward, inverse = [], []
    for name, side in (("b", HB), ("s", HS)):
        for part in (column_table(side), row_table(side)):
            forward += [jnp.asarray(a) for a in pair_of(part)]
        for part in (row_table(side), column_table(side)):
            inverse += [jnp.asarray(np.ascontiguousarray(a.T)) for a in pair_of(part)]
        tabs[f"p{name}_in"] = jnp.asarray(chunk_phase(side, "in"))
        tabs[f"p{name}_out"] = jnp.asarray(chunk_phase(side, "out"))
    tabs["table"] = tuple(forward + inverse)
    return tabs


def body(
    big_input,
    small_input,
    spectral_weight,
    point_weight,
    point_bias,
    big_cotangent,
    small_cotangent,
    big_live,
    small_live,
):
    dp = lax.axis_size("dp")
    tabs = tables()
    *results, pg_all, gathered = main_pass(
        dp,
        big_live,
        small_live,
        point_bias.T,
        jnp.transpose(point_weight, (0, 2, 1)),
        big_input,
        small_input,
        spectral_weight,
        big_cotangent,
        small_cotangent,
        tabs,
    )
    if ring_fits(dp):
        _, x2_all, dz_all, part = gathered
    else:
        x2_all, dz_all, pg_all = lax.all_gather((*gathered, pg_all), "dp")
        part = None
    samples = 2 * dp
    pixels = (HB * HB + HS * HS) * dp
    spec, point, bias, *results = tail_pass(
        x2_all, dz_all, pg_all, part, results, 1.0 / math.sqrt(samples), 1.0 / math.sqrt(pixels)
    )
    return (*results, spec, jnp.transpose(point, (0, 2, 1)), bias.T)


def solution(mesh):
    in_specs = (
        P("dp", "chan", None, None),
        P("dp", "chan", None, None),
        P(None, "chan", None, None, None),
        P("chan", None, None),
        P("chan", None),
        P("dp", "chan", None, None),
        P("dp", "chan", None, None),
        P("dp"),
        P("dp"),
    )
    out_specs = (
        P("dp", "chan", None, None),
        P("dp", "chan", None, None),
        P("dp", "chan", None, None),
        P("dp", "chan", None, None),
        P(None, "chan", None, None, None),
        P("chan", None, None),
        P("chan", None),
    )
    return jax.shard_map(body, mesh=mesh, in_specs=in_specs, out_specs=out_specs, check_vma=False)
```

```python
import functools
import math

import jax
import jax.numpy as jnp
import ml_dtypes
import numpy as np
from jax import lax
from jax.experimental import pallas as pl
from jax.experimental.pallas import tpu as pltpu
from jax.sharding import PartitionSpec as P

M = 16
MODES = 2 * M * M
HB = 96
HS = 64
CB = HB // 8
CS = HS // 8
LB = 8 * HB
LS = 8 * HS
NB = HB * HB // 4
NS = HS * HS // 4
NQ = NB + NS
TILES = 4
NEAR = 5
PG = 384
VMEM_LIMIT = 62 * 1024 * 1024

def mode_numbers():
    mode = np.arange(MODES)
    row = mode // M
    return np.where(row < M, row, row - 2 * M), mode % M


def pair_of(table):
    high = table.astype(ml_dtypes.bfloat16)
    return high, (table - high.astype(np.float64)).astype(ml_dtypes.bfloat16)


def column_table(side):
    cell, out = np.arange(8 * side), np.arange(8 * M)
    angle = np.outer(cell % side, out % M) % side * (2.0 * np.pi / side)
    same = np.equal.outer(cell // side, out // M)
    return np.concatenate([np.cos(angle) * same, -np.sin(angle) * same], axis=1)


def row_table(side):
    k, l = mode_numbers()
    row = np.arange(8 * M)
    angle = np.outer(row // M, k) % side * (2.0 * np.pi / side)
    same = np.equal.outer(row % M, l)
    cos, sin = np.cos(angle) * same, np.sin(angle) * same
    real = np.concatenate([cos, sin], axis=0).reshape(2 * 8 * M, TILES, 128)
    imag = np.concatenate([-sin, cos], axis=0).reshape(2 * 8 * M, TILES, 128)
    return np.stack([real, imag], axis=2).reshape(2 * 8 * M, 2 * MODES)


def chunk_phase(side, kind):
    k, l = mode_numbers()
    chunk = np.arange(side // 8)
    angle = (np.outer(8 * chunk, k) % side) * (2.0 * np.pi / side)
    scale = 1.0 / side if kind == "in" else np.where(l == 0, 1.0, 2.0) / (2.0 * M)
    return np.stack([np.cos(angle) * scale, np.sin(angle) * scale], axis=1).astype(np.float32)


def interleave(channels):
    table = np.zeros((4, 128, 256), ml_dtypes.bfloat16)
    for blade in range(4):
        for channel in range(channels):
            table[blade, channel, 4 * channel + blade] = 1
    return table


def split(value):
    high = value.astype(jnp.bfloat16)
    return high, (value - high.astype(jnp.float32)).astype(jnp.bfloat16)


def dot3(ah, al, bh, bl, dims=(((1,), (0,)), ((), ()))):
    dot = functools.partial(lax.dot_general, dimension_numbers=dims, preferred_element_type=jnp.float32)
    return dot(ah, bh) + (dot(ah, bl) + dot(al, bh))


NT = (((1,), (1,)), ((), ()))


def first_stage(h, l, th, tl, yh, yl, used):
    yh[used, :], yl[used, :] = split(dot3(h, l, th[...], tl[...]))


def forward_tile(yh, yl, vh, vl, phase, chunk0, count, rows, t):
    cols = pl.ds(pl.multiple_of(256 * t, 256), 256)
    used = slice(0, count * rows)
    local = dot3(yh[used, :], yl[used, :], vh[:, cols], vl[:, cols])
    lanes = pl.ds(pl.multiple_of(128 * t, 128), 128)
    re = im = None
    for j in range(count):
        lr = local[rows * j : rows * (j + 1), :128]
        li = local[rows * j : rows * (j + 1), 128:]
        cos = phase[chunk0 + j, 0:1, lanes]
        sin = phase[chunk0 + j, 1:2, lanes]
        pr = lr * cos + li * sin
        pi = li * cos - lr * sin
        re, im = (pr, pi) if re is None else (re + pr, im + pi)
    return re, im


def turn_modes(z_ref, zh, zl, phase, chunk, s, rows, row0):
    def tile(t, _):
        lanes = pl.ds(pl.multiple_of(128 * t, 128), 128)
        zr = z_ref[t, :, 256 * s : 256 * s + 128]
        zi = z_ref[t, :, 256 * s + 128 : 256 * s + 256]
        cos = phase[chunk, 0:1, lanes]
        sin = phase[chunk, 1:2, lanes]
        for part, value in enumerate((zr * cos - zi * sin, zr * sin + zi * cos)):
            high, low = split(value)
            where = pl.ds(pl.multiple_of(256 * t + 128 * part, 128), 128)
            zh[row0 : row0 + rows, where] = high
            zl[row0 : row0 + rows, where] = low
        return 0

    lax.fori_loop(0, TILES, tile, 0)


class Lanes:
    def __init__(self):
        sub = lax.broadcasted_iota(jnp.int32, (8, 128), 0)
        self.sub, self.s4 = sub, sub % 4
        self.even = sub % 2 == 0
        self.low = sub % 4 < 2
        self.half = sub < 4
        self.sign = jnp.where(self.even, 1.0, -1.0).astype(jnp.float32)
        self.sign_own = jnp.where(self.s4 == 1, -1.0, 1.0).astype(jnp.float32)
        self.sign_other = jnp.where(self.s4 == 2, -1.0, 1.0).astype(jnp.float32)
        self.by = {k: jnp.bitwise_xor(sub, k) for k in (1, 2, 3, 4)}

    def swap(self, x, k):
        return jnp.take_along_axis(x, self.by[k], axis=0)

    def to_matrix(self, x):
        return x * self.sign + self.swap(x, 1)

    def to_entries(self, x):
        return x * self.sign_own + self.swap(x, 1) * self.sign_other

    def columns(self, m):
        m3 = self.swap(m, 3)
        return jnp.where(self.even, m, m3), jnp.where(self.even, m3, m)


def mix_tile(wm, t, load, z_ref, me, xe, ln):
    groups = xe.shape[3] // 8
    outs = wm.shape[2]

    def expand(g, _):
        rows = pl.ds(pl.multiple_of(8 * g, 8), 8)
        for s in range(2):
            parts = []
            for ri in range(2):
                lanes = slice(256 * s + 128 * ri, 256 * s + 128 * ri + 128)
                parts.append(ln.columns(load(rows, lanes)))
            for c in range(2):
                xe[s, c, 0, rows, :] = parts[0][c]
                xe[s, c, 1, rows, :] = parts[1][c]
                xe[s, c, 2, rows, :] = parts[0][c] + parts[1][c]
        return 0

    lax.fori_loop(0, groups, expand, 0)

    def pair(p, _):
        acc = {}
        for g in range(groups):
            rows = slice(8 * g, 8 * g + 8)
            w = []
            for a in range(2):
                wr, wi = wm[t, 0, 2 * p + a, rows, :], wm[t, 1, 2 * p + a, rows, :]
                w.append((wr, wi, wr + wi))
            for s in range(2):
                for c in range(2):
                    for q in range(3):
                        x = xe[s, c, q, rows, :]
                        for a in range(2):
                            key = (a, s, c, q)
                            acc[key] = w[a][q] * x + acc[key] if key in acc else w[a][q] * x
        rows = pl.ds(pl.multiple_of(4 * outs * me + 8 * p, 8), 8)
        for s in range(2):
            for ri in range(2):
                out = []
                for a in range(2):
                    red = []
                    for c in range(2):
                        t1, t2, t3 = (acc[a, s, c, q] for q in range(3))
                        value = t1 - t2 if ri == 0 else t3 - t1 - t2
                        value = value + ln.swap(value, 4)
                        red.append(value + ln.swap(value, 2))
                    first = jnp.where(ln.low, red[0], red[1])
                    first = jnp.where(ln.even, first, ln.swap(first, 1))
                    second = jnp.where(ln.low, red[1], red[0])
                    second = jnp.where(ln.even, ln.swap(second, 1), second)
                    out.append(0.5 * (first + ln.sign * second))
                z_ref[t, rows, 256 * s + 128 * ri : 256 * s + 128 * ri + 128] = jnp.where(ln.half, out[0], out[1])
        return 0

    lax.fori_loop(0, outs // 2, pair, 0)


def both_outputs(d, ln):
    turned = ln.swap(d, 4)
    return jnp.where(ln.half, d, turned), jnp.where(ln.half, turned, d)


def unmix_tile(wm, t, d_ref, x_ref, de, ln):
    groups = x_ref.shape[1] // 8
    outs = wm.shape[2]

    def expand(p, _):
        rows = pl.ds(pl.multiple_of(8 * p, 8), 8)
        for s in range(2):
            vals = []
            for ri in range(2):
                m = ln.to_matrix(d_ref[t, rows, 256 * s + 128 * ri : 256 * s + 128 * ri + 128])
                vals.append(both_outputs(m, ln))
            for a in range(2):
                pats = []
                for ri in range(2):
                    m = vals[ri][a]
                    m2 = ln.swap(m, 2)
                    outer = (ln.s4 == 0) | (ln.s4 == 3)
                    pats.append((jnp.where(outer, m, m2), jnp.where(outer, m2, m)))
                for c in range(2):
                    here = pl.ds(pl.multiple_of(16 * p + 8 * a, 8), 8)
                    de[s, c, 0, here, :] = pats[0][c]
                    de[s, c, 1, here, :] = pats[1][c]
                    de[s, c, 2, here, :] = pats[0][c] + pats[1][c]
        return 0

    lax.fori_loop(0, outs // 2, expand, 0)

    def pair(p, _):
        acc = {}
        for o in range(outs):
            w = []
            for a in range(2):
                where = pl.ds(pl.multiple_of(16 * p + 8 * a, 8), 8)
                wr, wi = wm[t, 0, o, where, :], wm[t, 1, o, where, :]
                w.append((wr, wi, wr - wi))
            for s in range(2):
                for c in range(2):
                    for q in range(3):
                        d = de[s, c, q, 8 * o : 8 * o + 8, :]
                        for a in range(2):
                            key = (a, s, c, q)
                            acc[key] = w[a][q] * d + acc[key] if key in acc else w[a][q] * d
        for a in range(2):
            rows = pl.ds(pl.multiple_of(16 * p + 8 * a, 8), 8)
            for s in range(2):
                for ri in range(2):
                    red = []
                    for c in range(2):
                        t1, t2, t3 = (acc[a, s, c, q] for q in range(3))
                        value = t1 + t2 if ri == 0 else t3 - t1 + t2
                        red.append(value + ln.swap(value, 3))
                    q0, q1 = red
                    q0s, q1s = ln.swap(q0, 1), ln.swap(q1, 1)
                    f = jnp.where(ln.low, jnp.where(ln.even, q0, q0s), jnp.where(ln.even, q1s, q1))
                    h = jnp.where(ln.low, jnp.where(ln.even, q1s, q1), jnp.where(ln.even, q0, q0s))
                    x_ref[t, rows, 256 * s + 128 * ri : 256 * s + 128 * ri + 128] = 0.5 * (f + ln.sign * h)
        return 0

    lax.fori_loop(0, groups // 2, pair, 0)


def outer_expand(ln, outs, load, put):
    def one(p, _):
        for s in range(2):
            both = [both_outputs(ln.to_entries(load(p, s, ri)), ln) for ri in range(2)]
            for a in range(2):
                parts = [(both[ri][a], ln.swap(both[ri][a], 2)) for ri in range(2)]
                for r in range(2):
                    put(s, r, 0, 2 * p + a, parts[0][r])
                    put(s, r, 1, 2 * p + a, parts[1][r])
                    put(s, r, 2, 2 * p + a, parts[0][r] + parts[1][r])
        return 0

    lax.fori_loop(0, outs // 2, one, 0)


def outer_sums(devices, outs, groups, load_x, load_d, first, store, unroll):
    ob, kb = outs // 2, groups // 2

    def block(q, r, o0, k0):
        total = {}
        if first is not None:
            total = {(a, k): first(r, q, o0 + a, k0 + 8 * k) for a in range(ob) for k in range(kb)}
        for n in range(devices):
            for s in range(2):
                d = [load_d(n, s, r, q, o0 + a) for a in range(ob)]
                for k in range(kb):
                    x = load_x(n, s, q, k0 + 8 * k)
                    for a in range(ob):
                        total[a, k] = total[a, k] + d[a] * x if (a, k) in total else d[a] * x
        for (a, k), value in total.items():
            store(r, q, o0 + a, k0 + 8 * k, value)

    for q in range(3):
        if unroll:
            for r in range(2):
                for o0 in (0, ob):
                    for k0 in (0, 8 * kb):
                        block(q, r, o0, k0)
            continue

        def one(b, _):
            block(q, lax.rem(b, 2), lax.rem(lax.div(b, 2), 2) * ob, lax.div(b, 4) * (8 * kb))
            return 0

        lax.fori_loop(0, 8, one, 0)


def eight(row):
    return pl.ds(row if isinstance(row, int) else pl.multiple_of(row, 8), 8)


def outer_row(outs, rows, r, q, o, k):
    return ((r * 3 + q) * outs + o) * rows + k


def fold_point(pg, spread, rows, point, bias, scale):
    total = pg[0]
    for n in range(1, pg.shape[0]):
        total = total + pg[n]
    total = total * scale
    outs = total.shape[0] // 4
    for k in range(3):
        rows[k] = total[:, 128 * k : 128 * k + 128]
    blades = [None] * 4
    ones = jnp.ones((8, 128), jnp.bfloat16)
    for a in range(4):
        some = pl.ds(a, outs, stride=4)
        high, low = split(jnp.concatenate([rows[0, some, :], rows[1, some, :]], axis=1))
        for b in range(4):
            dot = functools.partial(lax.dot_general, dimension_numbers=NT, preferred_element_type=jnp.float32)
            value = dot(high, spread[b]) + dot(low, spread[b])
            value = -value if minus_sign(a, b) else value
            blades[a ^ b] = value if blades[a ^ b] is None else blades[a ^ b] + value
        high, low = split(rows[2, some, :])
        bias[a : a + 1, :] = (dot(ones, high) + dot(ones, low))[0:1, :]
    for c in range(4):
        point[:, c, :] = blades[c][:, : point.shape[2]]


def minus_sign(a, b):
    return b == (3 if a < 2 else 1)


def tail_kernel(scale, point_scale, steps, partial, x_ref, d_ref, pg, spread, *refs):
    part_ref, refs = (refs[0], refs[1:]) if partial else (None, refs)
    results, (g_ref, point, bias, *outs_ref), refs = refs[:4], refs[4:11], refs[11:]
    (acc, xd, de, rows3, sems), held = refs[:5], refs[5:]
    ln = Lanes()
    tile, side, step = pl.program_id(0), pl.program_id(1), pl.program_id(2)
    devices, rows = x_ref.shape[0], x_ref.shape[2]
    groups = rows // 8
    outs = d_ref.shape[2] // 4

    def load(i):
        return pltpu.make_async_copy(results[i], held[i], sems.at[0, i])

    def store(i):
        return pltpu.make_async_copy(held[i], outs_ref[i], sems.at[1, i])

    @pl.when((tile == 0) & (side == 0) & (step == 0))
    def _():
        for i in range(4):
            load(i).start()
        fold_point(pg, spread, rows3, point, bias, point_scale)

    @pl.when((tile == 1) & (side == 0) & (step == 0))
    def _():
        for i in range(4):
            load(i).wait()
            store(i).start()

    @pl.when((tile == TILES - 1) & (side == 1) & (step == steps - 1))
    def _():
        for i in range(4):
            store(i).wait()

    @pl.when((side == 0) | (steps > 1))
    def _():
        def expand(n, _):
            def put(s, r, q, o, value):
                de[n, s, r, q, o] = value

            outer_expand(
                ln, outs, lambda p, s, ri: d_ref[n, 0, eight(8 * p), 256 * s + 128 * ri : 256 * s + 128 * ri + 128], put
            )
            return 0

        lax.fori_loop(0, devices, expand, 0)

    def differ(n, _):
        for s in range(2):
            xd[n, s] = x_ref[n, 0, :, 256 * s : 256 * s + 128] - x_ref[n, 0, :, 256 * s + 128 : 256 * s + 256]
        return 0

    lax.fori_loop(0, devices, differ, 0)

    def load_x(n, s, q, row):
        if q == 2:
            return xd[n, s, eight(row), :]
        return x_ref[n, 0, eight(row), 256 * s + 128 * q : 256 * s + 128 * q + 128]

    def first(r, q, o, row):
        if partial:
            return part_ref[0, 0, eight(outer_row(outs, rows, r, q, o, row)), :]
        return jnp.where(step == 0, 0.0, acc[r, q, o, eight(row), :])

    def keep(r, q, o, row, value):
        acc[r, q, o, eight(row), :] = value

    outer_sums(
        devices,
        outs,
        groups,
        load_x,
        lambda n, s, r, q, o: de[n, s, r, q, o],
        first if partial or steps > 1 else None,
        keep,
        True,
    )

    @pl.when(step == steps - 1)
    def _():
        def finish(o, _):
            for g in range(groups):
                where = slice(8 * g, 8 * g + 8)
                for ri in range(2):
                    v = []
                    for r in range(2):
                        t1, t2 = acc[r, 0, o, where, :], acc[r, 1, o, where, :]
                        v.append(t1 + t2 if ri == 0 else acc[r, 2, o, where, :] - t1 + t2)
                    folded = jnp.where(ln.low, v[0], v[1]) + ln.swap(jnp.where(ln.low, v[1], v[0]), 3)
                    out = (folded * ln.sign + ln.swap(folded, 1)) * (0.5 * scale)
                    g_ref[ri, o, 2 * g : 2 * g + 2, :, :] = out.reshape(2, 4, 128)
            return 0

        lax.fori_loop(0, outs, finish, 0)


def tail_pass(x, d, pg, part, results, scale, point_scale):
    count, rows = x.shape[0], x.shape[2]
    own = d.shape[2]
    outs = own // 4
    group = count if count <= 8 else 8
    steps = count // group
    any_space = pl.BlockSpec(memory_space=pl.ANY)
    parts = [] if part is None else [part]
    return pl.pallas_call(
        functools.partial(tail_kernel, scale, point_scale, steps, part is not None),
        grid=(TILES, 2, steps),
        in_specs=[
            pl.BlockSpec((group, 1, rows // 2, 512), lambda t, h, n: (n, t, h, 0)),
            pl.BlockSpec((group, 1, own, 512), lambda t, h, n: (n, t, 0, 0)),
            pl.BlockSpec(pg.shape, lambda t, h, n: (0, 0, 0)),
            pl.BlockSpec((4, 128, 256), lambda t, h, n: (0, 0, 0)),
        ]
        + [pl.BlockSpec((1, 1, *p.shape[2:]), lambda t, h, n: (t, h, 0, 0)) for p in parts]
        + [any_space] * 4,
        out_specs=[
            pl.BlockSpec((2, outs, rows // 8, 4, 128), lambda t, h, n: (0, 0, h, 0, t)),
            pl.BlockSpec((outs, 4, rows // 4), lambda t, h, n: (0, 0, 0)),
            pl.BlockSpec((4, outs), lambda t, h, n: (0, 0)),
        ]
        + [any_space] * 4,
        out_shape=[
            jax.ShapeDtypeStruct((2, outs, rows // 4, 4, MODES), jnp.float32),
            jax.ShapeDtypeStruct((outs, 4, rows // 4), jnp.float32),
            jax.ShapeDtypeStruct((4, outs), jnp.float32),
        ]
        + [jax.ShapeDtypeStruct(r.shape, r.dtype) for r in results],
        scratch_shapes=[
            pltpu.VMEM((2, 3, outs, rows // 2, 128), jnp.float32),
            pltpu.VMEM((group, 2, rows // 2, 128), jnp.float32),
            pltpu.VMEM((group, 2, 2, 3, outs, 8, 128), jnp.float32),
            pltpu.VMEM((3, own, 128), jnp.float32),
            pltpu.SemaphoreType.DMA((2, 4)),
        ]
        + [pltpu.VMEM(r.shape, r.dtype) for r in results],
        compiler_params=pltpu.CompilerParams(vmem_limit_bytes=VMEM_LIMIT),
        cost_estimate=pl.CostEstimate(flops=600 << 20, bytes_accessed=46 << 20, transcendentals=0),
        name="tail_pass",
    )(x, d, pg, jnp.asarray(interleave(rows // 4)), *parts, *results)


MESH = pl.DeviceIdType.MESH


ERFC_SCALE = 0.282842712474619
ERFC = (
    0.11596259978194932,
    0.08090248108382336,
    0.23415924605220384,
    -0.1854802317493698,
    0.3545891457413051,
    -0.10013325473465298,
)


def normal_cdf(u):
    bell = jnp.exp(u * u * -0.5)
    t = 1.0 / (1.0 + ERFC_SCALE * jnp.abs(u))
    tail = ERFC[-1]
    for factor in ERFC[-2::-1]:
        tail = tail * t + factor
    tail = tail * t * bell
    return jnp.where(u >= 0.0, 1.0 - tail, tail), bell


def smem():
    return pl.BlockSpec(memory_space=pltpu.SMEM)


def vmem():
    return pl.BlockSpec(memory_space=pltpu.VMEM)


def grids():
    return ((LB, CB // 4, 0, NB), (LS, CS // 4, NB, NS))


def pieces():
    return [(s, j) for s, (_, count, _, _) in enumerate(grids()) for j in range(count)]


class Place:
    def __init__(self, count):
        self.me = lax.axis_index("chan")
        self.x = self.me // 2
        self.core = self.me % 2
        other, across = 1 - self.core, 1 - self.x
        self.peer = (2 * self.x + other, 2 * across + self.core, 2 * across + other)
        self.other_core, self.other_x = other, across
        self.count = count
        self.dp = lax.axis_index("dp")
        odd, pair = self.dp % 2, self.dp // 2
        self.pos = (1 - odd) * pair + odd * (count - 1 - pair)

    def at_pos(self, p):
        n = self.count
        p = (p + n) % n
        back = p // (n // 2)
        return (1 - back) * (2 * p) + back * (2 * (n - 1 - p) + 1)

    def copy(self, src, dst, send, recv, r):
        return pltpu.make_async_remote_copy(
            src_ref=src,
            dst_ref=dst,
            send_sem=send,
            recv_sem=recv,
            device_id={"chan": self.peer[r]},
            device_id_type=MESH,
        )

    def barrier(self):
        sem = pltpu.get_barrier_semaphore()
        for r in range(3):
            pl.semaphore_signal(sem, inc=1, device_id={"chan": self.peer[r]}, device_id_type=MESH)
        ring = ring_fits(self.count)
        for d in (1, -1) if ring else ():
            pl.semaphore_signal(sem, inc=1, device_id={"dp": self.at_pos(self.pos + d)}, device_id_type=MESH)
        pl.semaphore_wait(sem, 5 if ring else 3)


class ToCells:
    def __init__(self, here, big, small, dst, send, recv, local):
        self.here, self.srcs, self.dst, self.send, self.recv, self.local = here, (big, small), dst, send, recv, local

    def parts(self, s, j, who):
        width, count, first, cells = grids()[s]
        src = self.srcs[s].at[0, :, :, pl.ds(pl.multiple_of(cells * who + width * j, 128), width)]
        return src, self.dst.at[pl.ds(12 * self.here.me, 12), :, pl.ds(first + width * j, width)], s * grids()[0][1] + j

    def to(self, s, j, r):
        src, dst, k = self.parts(s, j, self.here.peer[r])
        return self.here.copy(src, dst, self.send.at[r, k], self.recv.at[r, k], r)

    def own(self, s, j):
        src, dst, k = self.parts(s, j, self.here.me)
        return pltpu.make_async_copy(src, dst, self.local.at[k])

    def across(self, s, j):
        for r in (1, 2):
            self.to(s, j, r).start()

    def near(self, s, j):
        self.to(s, j, 0).start()
        self.own(s, j).start()

    def arrived(self, s, j):
        self.own(s, j).wait()
        for r in range(3):
            self.to(s, j, r).wait_recv()

    def sent(self, s, j):
        for r in range(3):
            self.to(s, j, r).wait_send()


class ToChannels:
    def __init__(self, here, src, big, small, send, recv, local):
        self.here, self.src, self.dsts, self.send, self.recv, self.local = here, src, (big, small), send, recv, local

    def parts(self, s, j, who):
        width, count, first, cells = grids()[s]
        src = self.src.at[pl.ds(12 * who, 12), :, pl.ds(first + width * j, width)]
        lanes = pl.ds(pl.multiple_of(cells * self.here.me + width * j, 128), width)
        return src, self.dsts[s].at[0, :, :, lanes], s * grids()[0][1] + j

    def to(self, s, j, r):
        src, dst, k = self.parts(s, j, self.here.peer[r])
        return self.here.copy(src, dst, self.send.at[r, k], self.recv.at[r, k], r)

    def own(self, s, j):
        src, dst, k = self.parts(s, j, self.here.me)
        return pltpu.make_async_copy(src, dst, self.local.at[k])

    def start(self, s, j):
        for r in (1, 2, 0):
            self.to(s, j, r).start()
        self.own(s, j).start()


class Gather:
    def __init__(self, here, ref, send, recv, own):
        self.here, self.ref, self.send, self.recv, self.own = here, ref, send, recv, own

    def rows(self, t, who):
        return self.ref.at[t, pl.ds(pl.multiple_of(self.own * who, 8), self.own), :]

    def direct(self, t, r):
        block = self.rows(t, self.here.me)
        return self.here.copy(block, block, self.send.at[r, t], self.recv.at[r, t], r)

    def onward(self, t):
        block = self.rows(t, self.here.peer[1])
        return self.here.copy(block, block, self.send.at[2, t], self.recv.at[2, t], 0)

    def start(self, t):
        self.direct(t, 1).start()
        self.direct(t, 0).start()

    def forward(self, t):
        self.direct(t, 1).wait_recv()
        self.onward(t).start()

    def arrived(self, t):
        self.direct(t, 0).wait_recv()
        self.onward(t).wait_recv()

    def sent(self, t):
        self.direct(t, 0).wait_send()
        self.direct(t, 1).wait_send()
        self.onward(t).wait_send()


class SumAll:
    def __init__(self, here, part, first, second, total, send, recv, ln):
        self.here, self.part, self.first, self.second, self.total = here, part, first, second, total
        self.send, self.recv, self.ln = send, recv, ln
        self.half = part.shape[1] // 2

    def rows(self, core):
        return pl.ds(pl.multiple_of(self.half * core, 8), self.half)

    def step(self, k, s, t):
        lanes = pl.ds(256 * s, 256)
        sems = self.send.at[k, s, t], self.recv.at[k, s, t]
        if k == 0:
            src, dst = self.part.at[t, self.rows(self.here.other_core), lanes], self.first.at[t, :, lanes]
            return self.here.copy(src, dst, *sems, 0)
        if k == 1:
            return self.here.copy(self.first.at[t, :, lanes], self.second.at[t, :, lanes], *sems, 1)
        block = self.total.at[t, self.rows(self.here.core), lanes]
        return self.here.copy(block, block, *sems, 0)

    def across(self, s, t):
        self.step(0, s, t).wait()
        lanes = slice(256 * s, 256 * s + 256)
        self.first[t, :, lanes] = self.first[t, :, lanes] + self.part[t, self.rows(self.here.core), lanes]
        self.step(1, s, t).start()

    def back(self, s, t):
        self.step(1, s, t).wait_recv()
        ln = self.ln

        def group(g, _):
            rows = pl.ds(pl.multiple_of(8 * g, 8), 8)
            mine = pl.ds(pl.multiple_of(self.half * self.here.core + 8 * g, 8), 8)
            for ri in range(2):
                lanes = slice(256 * s + 128 * ri, 256 * s + 128 * ri + 128)
                self.total[t, mine, lanes] = ln.to_entries(self.first[t, rows, lanes] + self.second[t, rows, lanes])
            return 0

        lax.fori_loop(0, self.half // 8, group, 0)
        self.step(2, s, t).start()


class SumScatter:
    def __init__(self, here, part, first, second, result, send, recv, lead, width):
        self.here, self.part, self.first, self.second, self.result = here, part, first, second, result
        self.send, self.recv, self.lead, self.width = send, recv, lead, width
        self.own = result.shape[-2]

    def rows(self, ref, t, s, block):
        where = (pl.ds(pl.multiple_of(self.own * block, 8), self.own), pl.ds(self.width * s, self.width))
        return ref.at[(t, *where)] if self.lead else ref.at[where]

    def over(self, s, t, x):
        src = self.rows(self.part, t, s, 2 * x + self.here.other_core)
        return self.here.copy(src, self.rows(self.first, t, s, x), self.send.at[x, s, t], self.recv.at[x, s, t], 0)

    def across_copy(self, s, t):
        src, dst = self.rows(self.first, t, s, self.here.other_x), self.rows(self.second, t, s, 0)
        return self.here.copy(src, dst, self.send.at[2, s, t], self.recv.at[2, s, t], 1)

    def start(self, s, t):
        for x in range(2):
            self.over(s, t, x).start()

    def across(self, s, t):
        for x in range(2):
            self.over(s, t, x).wait_recv()
            slot = self.rows(self.first, t, s, x)
            slot[...] = slot[...] + self.rows(self.part, t, s, 2 * x + self.here.core)[...]
        self.across_copy(s, t).start()

    def finish(self, s, t):
        self.across_copy(s, t).wait_recv()
        result = self.rows(self.result, t, s, 0)
        result[...] = self.rows(self.first, t, s, self.here.x)[...] + self.rows(self.second, t, s, 0)[...]

    def sent(self, s, t):
        for x in range(2):
            self.over(s, t, x).wait_send()
        self.across_copy(s, t).wait_send()


class Ring:
    def __init__(self, here, streams, send, recv):
        self.here, self.streams, self.send, self.recv = here, streams, send, recv
        self.steps = here.count // 2 if ring_fits(here.count) else 0

    def origin(self, way, step):
        return self.here.at_pos(self.here.pos - (step + 1) * (1 - 2 * way))

    def part(self, way, step):
        return way if step == self.steps - 1 else None

    def copies(self, way, step):
        target = self.here.at_pos(self.here.pos + (1 - 2 * way))
        part = self.part(way, step)
        out = []
        for k, place in self.streams:
            out.append(
                pltpu.make_async_remote_copy(
                    src_ref=place(way, step - 1, part),
                    dst_ref=place(way, step, part),
                    send_sem=self.send.at[k, way, step],
                    recv_sem=self.recv.at[k, way, step],
                    device_id={"dp": target},
                    device_id_type=MESH,
                )
            )
        return out

    def start(self, step):
        for way in range(2):
            for cp in self.copies(way, step) if step < self.steps else ():
                cp.start()

    def advance(self, step, then):
        for way in range(2) if step <= self.steps else ():
            for cp in self.copies(way, step - 1):
                cp.wait_recv()
            for cp in self.copies(way, step) if step < self.steps else ():
                cp.start()
            for cp in then(way, step - 1):
                cp.start()

    def first_sent(self):
        for way in range(2) if self.steps else ():
            for cp in self.copies(way, 0):
                cp.wait_send()

    def finish(self, then, first=0, kept=0):
        for way in range(2):
            for step in range(self.steps):
                for cp in self.copies(way, step) if step >= first else ():
                    cp.wait_send()
                for cp in then(way, step) if step >= kept else ():
                    cp.wait()


def ring_fits(count):
    return count == 8


def spectral_piece(z_ref, zh, zl, yh, yl, pre, inverse, phase, chunk, count, s, rows, width):
    vth, vtl, wth, wtl = inverse
    for j in range(count):
        turn_modes(z_ref, zh, zl, phase, chunk + j, s, rows, rows * j)
    used = slice(0, count * rows)
    first_stage(zh[used, :], zl[used, :], vth, vtl, yh, yl, used)

    def tile(n, _):
        lanes = pl.ds(pl.multiple_of(256 * n, 256), 256)
        pre[used, lanes] = dot3(yh[used, :], yl[used, :], wth[:, lanes], wtl[:, lanes])
        return 0

    lax.fori_loop(0, width // 256, tile, 0)


def main_kernel(
    dp_count, live_big, live_small, bias_in, weights, spread, big, small, w, cbig, csmall, tables_in, phases,
    big_out, small_out, big_grad, small_grad, pg_all, gathered,
    tabs, vbuf, cbuf, ob, osm, gb, gs, kh, kl, sh, sl, x1, z1, x2, x2a, x2b, x2t, dza, dzb, dzo, dxo, xs, pgs,
    wm, xe, de, hid, zh, zl, yh, yl, pre, blades, c_own, c_all, square, ch, cl, dh, dl, pg, pga, pgb, pgo,
    load_sem, own_sem, half_sem, chalf_sem, w_sem, local_sem, out_sem, ctd_half_sem,
    v_send, v_recv, c_send, c_recv, o_send, o_recv, d_send, d_recv, p_send, p_recv,
    x1_send, x1_recv, z1_send, z1_recv, z2_send, z2_recv, x2_send, x2_recv,
    dz_send, dz_recv, dx_send, dx_recv, pg_send, pg_recv,
    xr_send, xr_recv, xc_send, xc_recv, dr_send, dr_recv, keep_sem, ready, near_sem, sums_sem,
):
    here = Place(dp_count)
    ln = Lanes()
    pbi, psi, pbo, pso = phases
    rows = x1.shape[1]
    own = rows // 4
    outs = own // 4
    groups = rows // 8
    forward = (tabs[0:4], tabs[4:8])
    inverse = (tabs[8:12], tabs[12:16])
    phase_in, phase_out = (pbi, psi), (pbo, pso)
    own_rows = pl.ds(pl.multiple_of(own * here.me, 8), own)
    loads = [pltpu.make_async_copy(src, dst, load_sem.at[i]) for i, (src, dst) in enumerate(zip(tables_in, tabs))]
    g_planes = [pltpu.make_async_copy(cbig, gb, own_sem.at[2]), pltpu.make_async_copy(csmall, gs, own_sem.at[3])]
    planes = [pltpu.make_async_copy(big, ob, own_sem.at[0]), pltpu.make_async_copy(small, osm, own_sem.at[1])]

    def w_copy(t):
        dst = wm.at[t].reshape(2, outs, rows // 4, 4, 128)
        return pltpu.make_async_copy(w.at[:, :, :, :, pl.ds(128 * t, 128)], dst, w_sem.at[t])

    def point_copy(r):
        return here.copy(c_own, c_all.at[own_rows, :], p_send.at[r], p_recv.at[r], r)

    live = (live_big[0].astype(jnp.float32), live_small[0].astype(jnp.float32))

    fields = ToCells(here, ob, osm, vbuf, v_send, v_recv, half_sem)
    grads = ToCells(here, gb, gs, cbuf, c_send, c_recv, chalf_sem)
    outputs = ToChannels(here, vbuf, big_out, small_out, o_send, o_recv, out_sem)
    backs = ToChannels(here, cbuf, ob, osm, d_send, d_recv, ctd_half_sem)
    x1_gather = Gather(here, x1, x1_send, x1_recv, own)
    z1_gather = Gather(here, z1, z1_send, z1_recv, own)
    z2 = x2
    z2_gather = Gather(here, z2, z2_send, z2_recv, own)
    x2_sum = SumAll(here, x2, x2a, x2b, x2t, x2_send, x2_recv, ln)
    dz_sum = SumScatter(here, x1, dza, dzb, dzo, dz_send, dz_recv, True, 256)
    dx_sum = SumScatter(here, z1, x2a, x2b, dxo, dx_send, dx_recv, True, 512)
    pg_sum = SumScatter(here, pg, pga, pgb, pgo, pg_send, pg_recv, False, PG)
    half_rows = pl.ds(pl.multiple_of(2 * own * here.core, 8), 2 * own)
    lanes_of = (pl.ds(0, 256), pl.ds(256, 256))

    last = dp_count // 2 - 1
    ring = ring_fits(dp_count)
    x2_near, x2_far, dz_far, sums_out = gathered if ring else (None,) * 4

    def far(way, k):
        return 2 if k == last else way

    def span(first, size, part):
        if part is None:
            return pl.ds(first, size)
        return pl.ds(first + part * (size // 2), size // 2)

    def half_span(part):
        size = 2 * own if part is None else own
        first = 2 * own * here.core + (0 if part is None else own * part)
        return pl.ds(pl.multiple_of(first, 8), size)

    def x2_place(s):
        def place(way, k, part):
            if k < 0:
                return x2t.at[:, half_span(part), lanes_of[s]]
            slot = k if k == last else 4 * way + k
            return xs.at[slot, :, span(0, 2 * own, part), lanes_of[s]]

        return place

    def dz_place(s):
        def place(way, k, part):
            if k < 0:
                return dzo.at[:, span(0, own, part), lanes_of[s]]
            ref = x2t if way == 0 or k == last else z2
            return ref.at[:, span(own * k, own, part), lanes_of[s]]

        return place

    def pg_place(way, k, part):
        if k < 0:
            return pgo.at[span(0, own, part), :]
        return pgs.at[k if k == last else 4 * way + k, span(0, own, part), :]

    x2_rings = [Ring(here, [(s, x2_place(s))], xr_send, xr_recv) for s in range(2)]
    dz_rings = [
        Ring(here, [(0, dz_place(0))], dr_send, dr_recv),
        Ring(here, [(1, dz_place(1)), (2, pg_place)], dr_send, dr_recv),
    ]

    def keep_x2(s):
        def keep(way, k):
            part = x2_rings[s].part(way, k)
            slot = x2_place(s)(way, k, part)
            ref = x2_near.at[1 + 2 * k + way] if k < 2 else x2_far.at[far(way, k)]
            block = ref.at[:, half_span(part), lanes_of[s]]
            return (
                here.copy(slot, block, xc_send.at[s, way, k], xc_recv.at[s, way, k], 0),
                pltpu.make_async_copy(slot, block, keep_sem.at[s, way, k]),
            )

        return keep

    def keep_dz(s):
        def keep(way, k):
            ring = dz_rings[s]
            i, part = ring.origin(way, k), ring.part(way, k)
            out = []
            if k > 1:
                block = dz_far.at[far(way, k), :, span(0, own, part), lanes_of[s]]
                out.append(pltpu.make_async_copy(dz_place(s)(way, k, part), block, keep_sem.at[2 + s, way, k]))
            if s == 1:
                block = pg_all.at[i, span(0, own, part), :]
                out.append(pltpu.make_async_copy(pg_place(way, k, part), block, keep_sem.at[4, way, k]))
            return out

        return keep

    def x2_done():
        for s in range(2):
            for way in range(2):
                for k in range(2):
                    for cp in keep_x2(s)(way, k):
                        cp.wait()

    def x2_advance(s, step):
        x2_rings[s].advance(step, keep_x2(s))

    def dz_advance(s, step):
        dz_rings[s].advance(step, keep_dz(s))

    def tell_ready(s):
        if ring_fits(dp_count):
            x2_rings[s].first_sent()
            for way in range(2):
                target = here.at_pos(here.pos + (1 - 2 * way))
                pl.semaphore_signal(ready.at[s], inc=1, device_id={"dp": target}, device_id_type=MESH)

    def dz_start(s):
        if ring_fits(dp_count):
            pl.semaphore_wait(ready.at[s], 2)
            dz_rings[s].start(0)

    for cp in planes + loads[:8]:
        cp.start()
    here.barrier()
    for cp in planes:
        cp.wait()
    for j in range(CS // 4):
        fields.across(1, j)
    for s, j in pieces():
        fields.near(s, j)
    for t in range(TILES):
        w_copy(t).start()
    for cp in loads[8:] + g_planes:
        cp.start()
    for cp in loads[:8]:
        cp.wait()

    for ref, h, l, count, width in ((ob, kh, kl, CB, LB), (osm, sh, sl, CS, LS)):

        def stack(c, _):
            high, low = split(ref[0, :, :, pl.ds(pl.multiple_of(width * c, 128), width)].reshape(own, width))
            where = pl.ds(pl.multiple_of(own * c, 16), own)
            h[where, :] = high
            l[where, :] = low
            return 0

        lax.fori_loop(0, count, stack, 0)

    def own_modes(s):
        h, l, phase, count = ((kh, kl, pbi, CB), (sh, sl, psi, CS))[s]
        wh, wl, vh, vl = forward[s]
        first_stage(h[...], l[...], wh, wl, yh, yl, slice(0, count * own))

        def own_tile(t, _):
            re, im = forward_tile(yh, yl, vh, vl, phase, 0, count, own, t)
            x1[t, own_rows, 256 * s : 256 * s + 128] = re
            x1[t, own_rows, 256 * s + 128 : 256 * s + 256] = im
            if s == 0:
                x1_gather.start(t)
            return 0

        lax.fori_loop(0, TILES, own_tile, 0)

    own_modes(1)
    own_modes(0)
    blades[...] = jnp.zeros_like(blades)
    blades[0, :, : rows // 4] = weights[...].reshape(own, rows // 4)
    dense = jnp.zeros((own, 256), jnp.float32)
    for b in range(4):
        for g in range(own // 8):
            value = blades[0, 8 * g : 8 * g + 8, :]
            value = ln.swap(value, b) if b else value
            minus = (ln.s4 < 2) if b == 3 else (ln.s4 >= 2) if b == 1 else None
            blades[1, 8 * g : 8 * g + 8, :] = value if minus is None else jnp.where(minus, -value, value)
        high, low = split(blades[1])
        dense += jnp.dot(high, spread[b], preferred_element_type=jnp.float32)
        dense += jnp.dot(low, spread[b], preferred_element_type=jnp.float32)
    c_own[:, :256] = dense
    row = lax.broadcasted_iota(jnp.int32, (own, PG - 256), 0)
    column = jnp.zeros((own, PG - 256), jnp.float32)
    for o in range(outs):
        for a in range(4):
            column = jnp.where(row == 4 * o + a, bias_in[a, o], column)
    c_own[:, 256:] = column
    c_all[own_rows, :] = c_own[...]
    for r in range(3):
        point_copy(r).start()

    for t in range(TILES):
        w_copy(t).wait()

        def convert(i, _):
            ri, o = lax.rem(i, 2), lax.div(i, 2)
            for g in range(groups):
                where = slice(8 * g, 8 * g + 8)
                wm[t, ri, o, where, :] = ln.to_matrix(wm[t, ri, o, where, :])
            return 0

        lax.fori_loop(0, 2 * outs, convert, 0)
        x1_gather.forward(t)

    def mix_first(t, _):
        x1_gather.arrived(t)
        mix_tile(wm, t, lambda where, lanes: ln.to_entries(x1[t, where, lanes]), z1, here.me, xe, ln)
        z1_gather.start(t)

        @pl.when(t >= 1)
        def _():
            z1_gather.forward(t - 1)

        return 0

    lax.fori_loop(0, TILES, mix_first, 0)
    for cp in g_planes:
        cp.wait()
    z1_gather.forward(TILES - 1)
    for j in range(CB // 4):
        fields.across(0, j)
    grads.across(0, 0)
    for s, j in pieces():
        grads.near(s, j)
    for r in range(3):
        point_copy(r).wait_recv()
    square[0:rows, :] = c_all[:, :256]
    square[rows:256, :] = jnp.zeros((256 - rows, 256), jnp.float32)
    ch[...], cl[...] = split(c_all[:, :rows])
    dh[...], dl[...] = split(jnp.transpose(square[...])[:rows, :rows])

    for cp in loads[8:]:
        cp.wait()

    def pointwise(s, j, load, store):
        width, count, first, cells_here = grids()[s]

        def cells(n, _):
            lanes = pl.ds(pl.multiple_of(first + j * width + 256 * n, 256), 256)
            vh, vl = split(load(lanes))
            store(lanes, dot3(ch[...], cl[...], vh, vl) + c_all[:, 256:257])
            return 0

        lax.fori_loop(0, width // 256, cells, 0)

    def load_field(lanes):
        return vbuf[:, :, lanes].reshape(rows, 256)

    def store_field(lanes, value):
        vbuf[:, :, lanes] = value.reshape(rows // 4, 4, 256)

    def load_hid(lanes):
        return hid[:, lanes]

    def store_hid(lanes, value):
        hid[:, lanes] = value

    def point_piece(s, j):
        fields.arrived(s, j)
        pointwise(s, j, load_field, store_hid)

    for j in range(CS // 4):
        point_piece(1, j)

    def z1_arrived(t, _):
        z1_gather.arrived(t)
        return 0

    lax.fori_loop(0, TILES, z1_arrived, 0)

    def each_tile(fn):
        def one(t, _):
            fn(t)
            return 0

        lax.fori_loop(0, TILES, one, 0)

    for s, (width, count, first, cells_here) in enumerate(grids()):
        wh, wl, vh, vl = forward[s]
        chunk = here.me * count
        spectral_piece(z1, zh, zl, yh, yl, pre, inverse[s], phase_out[s], chunk, count, s, rows, width)
        if s == 1:
            each_tile(lambda t: x2_sum.across(0, t))
        for j in range(count):
            if s == 0:
                point_piece(0, j)

            def cells(n, _):
                at = pl.ds(pl.multiple_of(256 * n, 256), 256)
                lanes = pl.ds(pl.multiple_of(first + j * width + 256 * n, 256), 256)
                u = pre[rows * j : rows * (j + 1), at] + hid[:, lanes]
                out = load_field(lanes) + u * normal_cdf(u)[0]
                hid[:, lanes] = out
                oh, ol = split(out)
                kh[rows * j : rows * (j + 1), at] = oh
                kl[rows * j : rows * (j + 1), at] = ol
                return 0

            lax.fori_loop(0, width // 256, cells, 0)
        if s == 1:
            each_tile(lambda t: x2_sum.back(0, t))
            x2_rings[0].start(0)

        used = slice(0, count * rows)
        first_stage(kh[used, :width], kl[used, :width], wh, wl, yh, yl, used)

        def modes(t, _):
            re, im = forward_tile(yh, yl, vh, vl, phase_in[s], chunk, count, rows, t)
            x2[t, :, 256 * s : 256 * s + 128] = re
            x2[t, :, 256 * s + 128 : 256 * s + 256] = im
            x2_sum.step(0, s, t).start()
            return 0

        lax.fori_loop(0, TILES, modes, 0)
    for s, j in pieces():
        fields.sent(s, j)
    each_tile(lambda t: x2_sum.across(1, t))
    each_tile(lambda t: x2_sum.back(1, t))
    x2_rings[1].start(0)

    def crossed(t):
        for s in range(2):
            x2_sum.step(1, s, t).wait_send()

    each_tile(crossed)

    def mix_second(t, _):
        for s in range(2):
            x2_sum.step(2, s, t).wait_recv()
        mix_tile(wm, t, lambda where, lanes: x2t[t, where, lanes], z2, here.me, xe, ln)
        z2_gather.start(t)

        @pl.when(t >= 1)
        def _():
            z2_gather.forward(t - 1)

        return 0

    lax.fori_loop(0, TILES // 2, mix_second, 0)
    x2_advance(0, 1)
    lax.fori_loop(TILES // 2, TILES, mix_second, 0)
    x2_local = pltpu.make_async_copy(x2t, x2_near.at[0] if ring else gathered[0], local_sem.at[0])
    x2_local.start()
    z2_gather.forward(TILES - 1)
    grads.across(0, 1)
    grads.across(0, 2)
    for j in range(CS // 4):
        grads.across(1, j)
    for s, j in pieces():
        pointwise(s, j, load_hid, store_field)
    x2_advance(1, 1)
    each_tile(z2_gather.arrived)
    x2_advance(0, 2)
    each_tile(x1_gather.sent)
    each_tile(z1_gather.sent)
    pg[...] = jnp.zeros_like(pg)

    for s, (width, count, first, cells_here) in enumerate(grids()):
        wh, wl, vh, vl = forward[s]
        chunk = here.me * count
        spectral_piece(z2, zh, zl, yh, yl, pre, inverse[s], phase_out[s], chunk, count, s, rows, width)
        if s == 0:
            x2_local.wait()
            each_tile(z2_gather.sent)
        each_tile(lambda t: x2_sum.step(2, s, t).wait_send())
        tell_ready(s)
        if s == 1:
            each_tile(lambda t: dz_sum.across(0, t))
            backs.start(0, 0)
        for j in range(count):
            grads.arrived(s, j)

            def cells(n, _):
                at = pl.ds(pl.multiple_of(256 * n, 256), 256)
                lanes = pl.ds(pl.multiple_of(first + j * width + 256 * n, 256), 256)
                value = hid[:, lanes]
                vh, vl = split(value)
                u = pre[rows * j : rows * (j + 1), at] + load_field(lanes)
                cdf, bell = normal_cdf(u)
                store_field(lanes, value + u * cdf)
                slope = cdf + u * (bell * (1.0 / math.sqrt(2.0 * math.pi)))
                grad = cbuf[:, :, lanes].reshape(rows, 256) * live[s] * slope
                gh, gl = split(grad)
                kh[rows * j : rows * (j + 1), at] = gh
                kl[rows * j : rows * (j + 1), at] = gl
                cbuf[:, :, lanes] = dot3(dh[...], dl[...], gh, gl).reshape(rows // 4, 4, 256)
                pg[:, :rows] += dot3(gh, gl, vh, vl, NT)
                pg[:, 256:] += grad[:, :128] + grad[:, 128:]
                return 0

            lax.fori_loop(0, width // 256, cells, 0)
            if (s, j) == (0, 1):
                x2_advance(1, 2)
        if s == 1:
            each_tile(lambda t: dz_sum.finish(0, t))
            dz_start(0)

        used = slice(0, count * rows)
        first_stage(kh[used, :width], kl[used, :width], wh, wl, yh, yl, used)

        def modes(t, _):
            re, im = forward_tile(yh, yl, vh, vl, phase_out[s], chunk, count, rows, t)
            x1[t, :, 256 * s : 256 * s + 128] = re
            x1[t, :, 256 * s + 128 : 256 * s + 256] = im
            dz_sum.start(s, t)
            return 0

        lax.fori_loop(0, TILES, modes, 0)
        x2_advance(s, 3)
    pg_sum.start(0, 0)
    each_tile(lambda t: dz_sum.across(1, t))
    pg_sum.across(0, 0)
    backs.start(0, 1)
    backs.start(0, 2)
    for j in range(CS // 4):
        backs.start(1, j)
    each_tile(lambda t: dz_sum.finish(1, t))
    pg_sum.finish(0, 0)
    dz_start(1)
    dz_local = [pltpu.make_async_copy(pgo, pg_all.at[here.dp] if ring else pg_all, local_sem.at[2])]
    if not ring:
        dz_local.append(pltpu.make_async_copy(dzo, gathered[1], local_sem.at[1]))
    for cp in dz_local:
        cp.start()

    for t in range(TILES):
        unmix_tile(wm, t, dzo, z1, xe, ln)
        dx_sum.start(0, t)
        if t >= 1:
            dx_sum.across(0, t - 1)
        if t == 1:
            dz_advance(0, 1)
    dx_sum.across(0, TILES - 1)
    for s, j in pieces():
        outputs.start(s, j)
    dz_advance(1, 1)
    dz_advance(0, 2)

    flat = wm.reshape(TILES * 2 * outs * rows, 128)
    half = rows // 2
    acc_rows = 6 * outs * half
    xd_row0 = 2 * acc_rows

    def x_near(i):
        t, h = lax.div(i, 2), lax.rem(i, 2)
        out = []
        for n in range(NEAR):
            src = x2_near.at[n, t, pl.ds(pl.multiple_of(half * h, 8), half), :]
            dst = hid.at[pl.ds(pl.multiple_of(half * h, 8), half), pl.ds(512 * n, 512)]
            out.append(pltpu.make_async_copy(src, dst, near_sem.at[h, n]))
        return out

    def sums_copy(i):
        t, h = lax.div(i, 2), lax.rem(i, 2)
        src = flat.at[pl.ds(pl.multiple_of(acc_rows * h, 8), acc_rows), :]
        return pltpu.make_async_copy(src, sums_out.at[t, h], sums_sem.at[h])

    def de_at(n, s, r, q, o):
        return eight(((((n * 2 + s) * 2 + r) * 3 + q) * outs + o) * 8)

    def near_step(i, _):
        t, h = lax.div(i, 2), lax.rem(i, 2)
        for cp in x_near(i):
            cp.wait()

        @pl.when(i + 1 < 2 * TILES)
        def _():
            for cp in x_near(i + 1):
                cp.start()

        @pl.when(i >= 2)
        def _():
            sums_copy(i - 2).wait()

        @pl.when(h == 0)
        def _():
            for n, (ref, row0) in enumerate(((dzo, 0), (x2t, 0), (z2, 0), (x2t, own), (z2, own))):

                def put(s, r, q, o, value):
                    de[de_at(n, s, r, q, o), :] = value

                outer_expand(
                    ln, outs, lambda p, s, ri: ref[t, eight(row0 + 8 * p), 256 * s + 128 * ri : 256 * s + 128 * ri + 128], put
                )

        def x_row(row):
            return eight(h * half + row)

        def differ(g, _):
            for n in range(NEAR):
                for s in range(2):
                    x = hid[x_row(8 * g), 512 * n + 256 * s : 512 * n + 256 * s + 256]
                    flat[eight(xd_row0 + (n * 2 + s) * half + 8 * g), :] = x[:, :128] - x[:, 128:]
            return 0

        lax.fori_loop(0, half // 8, differ, 0)

        def load_x(n, s, q, row):
            if q == 2:
                return flat[eight(xd_row0 + (n * 2 + s) * half + row), :]
            lane = 512 * n + 256 * s + 128 * q
            return hid[x_row(row), lane : lane + 128]

        def keep_sum(r, q, o, row, value):
            flat[eight(acc_rows * h + outer_row(outs, half, r, q, o, row)), :] = value

        outer_sums(
            NEAR, outs, half // 8, load_x, lambda n, s, r, q, o: de[de_at(n, s, r, q, o), :], None, keep_sum, False
        )
        sums_copy(i).start()
        return 0

    def near_products(lo, hi):
        if ring:
            lax.fori_loop(lo, hi, near_step, 0)

    if ring:
        x2_done()
        for cp in x_near(0):
            cp.start()
        dz_advance(1, 2)
    near_products(0, 2)
    dz_advance(0, 3)
    near_products(2, 4)
    each_tile(lambda t: dx_sum.finish(0, t))
    dz_advance(1, 3)

    for s, (g, o, dst, phase, count, width) in enumerate(
        ((gb, ob, big_grad, pbi, CB, LB), (gs, osm, small_grad, psi, CS, LS))
    ):
        vth, vtl, wth, wtl = inverse[s]
        for j in range(count):
            turn_modes(dxo, zh, zl, phase, j, s, own, own * j)
        for j in range(count // 4):
            backs.own(s, j).wait()
            for r in range(3):
                backs.to(s, j, r).wait_recv()
        used = slice(0, count * own)
        first_stage(zh[used, :], zl[used, :], vth, vtl, yh, yl, used)

        def tile(n, _):
            lanes = pl.ds(pl.multiple_of(256 * n, 256), 256)
            part = dot3(yh[used, :], yl[used, :], wth[:, lanes], wtl[:, lanes])
            for j in range(count):
                where = pl.ds(pl.multiple_of(width * j + 256 * n, 256), 256)
                o[0, :, :, where] = (
                    part[own * j : own * (j + 1)].reshape(outs, 4, 256) + g[0, :, :, where] * live[s] + o[0, :, :, where]
                )
            return 0

        lax.fori_loop(0, width // 256, tile, 0)
        if s == 0:
            near_products(4, 6)
        pltpu.make_async_copy(o, dst, local_sem.at[3 + s]).start()
    near_products(6, 8)
    for s in range(2):
        x2_advance(s, 4)
        dz_advance(s, 4)

    for cp in dz_local:
        cp.wait()
    pltpu.make_async_copy(ob, big_grad, local_sem.at[3]).wait()
    pltpu.make_async_copy(osm, small_grad, local_sem.at[4]).wait()
    for r in range(3):
        point_copy(r).wait_send()
    for s, j in pieces():
        grads.sent(s, j)
        for r in range(3):
            backs.to(s, j, r).wait_send()
        outputs.own(s, j).wait()
        for r in range(3):
            outputs.to(s, j, r).wait()

    def last_tile(t, _):
        for s in range(2):
            dz_sum.sent(s, t)
        dx_sum.sent(0, t)
        return 0

    lax.fori_loop(0, TILES, last_tile, 0)
    pg_sum.sent(0, 0)
    for i in range(2 * TILES - 2, 2 * TILES) if ring else ():
        sums_copy(i).wait()
    for s in range(2):
        x2_rings[s].finish(keep_x2(s), 1, 2)
        dz_rings[s].finish(keep_dz(s))


def main_pass(dp, live_big, live_small, bias, weights, big, small, w, cbig, csmall, tabs):
    rows = w.shape[2] * 4
    outs = w.shape[1]
    own = rows // 4
    any_space = pl.BlockSpec(memory_space=pl.ANY)
    table = tabs["table"]
    phases = (tabs["pb_in"], tabs["ps_in"], tabs["pb_out"], tabs["ps_out"])
    f32, bf16 = jnp.float32, jnp.bfloat16

    def buf(*shape, dtype=f32):
        return pltpu.VMEM(shape, dtype)

    def dma(*shape):
        return pltpu.SemaphoreType.DMA(shape)

    modes = (TILES, rows, 512)
    half, quarter = (TILES, rows // 2, 512), (TILES, own, 512)
    ring = ring_fits(dp)
    steps = max(1, dp // 2) if ring else 1
    slots = 7 if ring else 1
    lead = (dp,) if ring else ()
    if ring:
        shapes = ((NEAR, *modes), (dp - NEAR, *modes), (dp - NEAR, *quarter), (TILES, 2, 3 * outs * rows, 128))
    else:
        shapes = (modes, quarter)
    gathered = tuple(jax.ShapeDtypeStruct(shape, f32) for shape in shapes)
    chunks = (CB + CS) // 4
    return pl.pallas_call(
        functools.partial(main_kernel, dp),
        in_specs=[smem()] * 3 + [vmem()] * 2 + [any_space] * 5 + [(any_space,) * len(table), (vmem(),) * 4],
        out_specs=[any_space] * 5 + [tuple(any_space for _ in gathered)],
        out_shape=[
            jax.ShapeDtypeStruct(big.shape, f32),
            jax.ShapeDtypeStruct(small.shape, f32),
            jax.ShapeDtypeStruct(big.shape, f32),
            jax.ShapeDtypeStruct(small.shape, f32),
            jax.ShapeDtypeStruct((*lead, own, PG), f32),
            gathered,
        ],
        scratch_shapes=[
            tuple(pltpu.VMEM(a.shape, bf16) for a in table),
            buf(rows // 4, 4, NQ),
            buf(rows // 4, 4, NQ),
            buf(*big.shape),
            buf(*small.shape),
            buf(*big.shape),
            buf(*small.shape),
            buf(own * CB, LB, dtype=bf16),
            buf(own * CB, LB, dtype=bf16),
            buf(own * CS, LS, dtype=bf16),
            buf(own * CS, LS, dtype=bf16),
            buf(*modes),
            buf(*modes),
            buf(*modes),
            buf(*half),
            buf(*half),
            buf(*modes),
            buf(*half),
            buf(*quarter),
            buf(*quarter),
            buf(*quarter),
            buf(slots, *half),
            buf(slots, own, PG),
            buf(TILES, 2, outs, rows, 128),
            buf(2, 2, 3, rows, 128),
            buf(NEAR * 12 * outs * 8 if ring else 8, 128),
            buf(rows, NQ),
            buf(own * CB, 2 * MODES, dtype=bf16),
            buf(own * CB, 2 * MODES, dtype=bf16),
            buf(own * CB, 256, dtype=bf16),
            buf(own * CB, 256, dtype=bf16),
            buf(own * CB, LB),
            buf(2, own, 128),
            buf(own, PG),
            buf(rows, PG),
            buf(256, 256),
            buf(rows, rows, dtype=bf16),
            buf(rows, rows, dtype=bf16),
            buf(rows, rows, dtype=bf16),
            buf(rows, rows, dtype=bf16),
            buf(rows, PG),
            buf(2 * own, PG),
            buf(own, PG),
            buf(own, PG),
            dma(len(table)),
            dma(4),
            dma(chunks),
            dma(chunks),
            dma(TILES),
            dma(5),
            dma(chunks),
            dma(chunks),
        ]
        + [dma(3, chunks)] * 8
        + [dma(3)] * 2
        + [dma(3, TILES)] * 6
        + [dma(3, 2, TILES)] * 2
        + [dma(3, 2, TILES)] * 2
        + [dma(3, 1, TILES)] * 2
        + [dma(3, 1, 1)] * 2
        + [dma(2, 2, steps)] * 4
        + [dma(3, 2, steps)] * 2
        + [dma(5, 2, steps), pltpu.SemaphoreType.REGULAR((2,)), dma(2, NEAR), dma(2)],
        compiler_params=pltpu.CompilerParams(vmem_limit_bytes=VMEM_LIMIT, collective_id=0, has_side_effects=True),
        cost_estimate=pl.CostEstimate(flops=40 << 30, bytes_accessed=60 << 20, transcendentals=0),
        name="main_pass",
    )(live_big, live_small, bias, weights, jnp.asarray(interleave(rows // 4)), big, small, w, cbig, csmall, table, phases)


def tables():
    tabs = {}
    forward, inverse = [], []
    for name, side in (("b", HB), ("s", HS)):
        for part in (column_table(side), row_table(side)):
            forward += [jnp.asarray(a) for a in pair_of(part)]
        for part in (row_table(side), column_table(side)):
            inverse += [jnp.asarray(np.ascontiguousarray(a.T)) for a in pair_of(part)]
        tabs[f"p{name}_in"] = jnp.asarray(chunk_phase(side, "in"))
        tabs[f"p{name}_out"] = jnp.asarray(chunk_phase(side, "out"))
    tabs["table"] = tuple(forward + inverse)
    return tabs


def body(
    big_input,
    small_input,
    spectral_weight,
    point_weight,
    point_bias,
    big_cotangent,
    small_cotangent,
    big_live,
    small_live,
):
    dp = lax.axis_size("dp")
    tabs = tables()
    *results, pg_all, gathered = main_pass(
        dp,
        big_live,
        small_live,
        point_bias.T,
        jnp.transpose(point_weight, (0, 2, 1)),
        big_input,
        small_input,
        spectral_weight,
        big_cotangent,
        small_cotangent,
        tabs,
    )
    if ring_fits(dp):
        _, x2_all, dz_all, part = gathered
    else:
        x2_all, dz_all, pg_all = lax.all_gather((*gathered, pg_all), "dp")
        part = None
    samples = 2 * dp
    pixels = (HB * HB + HS * HS) * dp
    spec, point, bias, *results = tail_pass(
        x2_all, dz_all, pg_all, part, results, 1.0 / math.sqrt(samples), 1.0 / math.sqrt(pixels)
    )
    return (*results, spec, jnp.transpose(point, (0, 2, 1)), bias.T)


def solution(mesh):
    in_specs = (
        P("dp", "chan", None, None),
        P("dp", "chan", None, None),
        P(None, "chan", None, None, None),
        P("chan", None, None),
        P("chan", None),
        P("dp", "chan", None, None),
        P("dp", "chan", None, None),
        P("dp"),
        P("dp"),
    )
    out_specs = (
        P("dp", "chan", None, None),
        P("dp", "chan", None, None),
        P("dp", "chan", None, None),
        P("dp", "chan", None, None),
        P(None, "chan", None, None, None),
        P("chan", None, None),
        P("chan", None),
    )
    return jax.shard_map(body, mesh=mesh, in_specs=in_specs, out_specs=out_specs, check_vma=False)
```
